128 devices in a mesh: blk: 8 (over y, x_lo), rep: 16 (over z, x_hi, core).
Axes of the slice: x: 4 (x_hi: 2, x_lo: 2; x = x_hi * 2 + x_lo), y: 4, z: 4, core: 2. Of those that a mesh axis runs over, the one named last changes fastest.
Arguments:
- image_feats: bfloat16 [16, 4096, 1024], P('rep', 'blk'), may hold values from -6 to 6
- text_feats: bfloat16 [16, 4096, 768], P('rep', 'blk'), may hold values from -6 to 6
- image_head: bfloat16 [1024, 768], replicated, may hold values from -0.1875 to 0.1875
- text_head: bfloat16 [768, 768], replicated, may hold values from -0.21875 to 0.21875
- image_lse: float32 [16, 4096], P('rep', 'blk'), as said below
- text_lse: float32 [16, 4096], P('rep', 'blk'), as said below
Outputs:
- image_feat_grad: float32 [16, 4096, 1024], P('rep', 'blk')
- text_feat_grad: float32 [16, 4096, 768], P('rep', 'blk')
- image_head_grad: float32 [1024, 768], replicated
- text_head_grad: float32 [768, 768], replicated
The draws below stay inside these ranges and needn't reach their ends.
Inputs may be any that keep to these rules, and one draw needn't show every extreme that they name: `image_lse`: each entry lies between ln(4096) + 1 and ln(4096) + 2.5. `text_lse`: each entry lies between ln(4096) + 1 and ln(4096) + 2.5.
All inputs are finite; a program needn't handle non-finite values.
Results may differ from the reference program's by a relative error of at most 0.028.
Values may be sent and summed in bfloat16 or wider, within the bound.
No kernel may reach another device: no remote copies, remote signals or barrier semaphores. Data moves between devices by JAX's collectives and lax.ppermute only.
A program may use at most 128 MiB of HBM per device.

```python
import jax
import jax.numpy as jnp
from jax import lax

EMBED = 768
VIS_WIDTH = 1024
TXT_WIDTH = 768
PAIRS = 4096
GROUPS = 16


def normalizer_values(key, salt):
    base = jax.random.fold_in(key, salt)
    lowest = jnp.log(jnp.float32(PAIRS)) + 1.0
    pick = jax.random.uniform(jax.random.fold_in(base, 1), (GROUPS, PAIRS), jnp.float32)
    offset = 1.5 * pick
    return lowest + offset


def draw_image_lse(key, part):
    return normalizer_values(key, 11)


def draw_text_lse(key, part):
    return normalizer_values(key, 23)


def shard_levels(key, extent, cuts, least, largest):
    level, own = 1.0, jax.random.fold_in(key, 6)
    for dim, parts in cuts:
        heights = jnp.exp(jax.random.uniform(jax.random.fold_in(own, dim), (parts,), jnp.float32, least / len(cuts), largest / len(cuts)))
        level = level * jnp.repeat(heights, extent[dim] // parts).reshape([-1 if axis == dim else 1 for axis in range(len(extent))])
    return level


def normal_values(key, shape, scale, bound, pieces=(), held_as=jnp.bfloat16):
    result = jax.random.normal(key, shape, jnp.float32) * scale
    if len(pieces) > 0:
        result = shard_levels(key, shape, pieces, -0.22, 0.18) * result
    return jnp.clip(result, min=-bound, max=bound).astype(held_as)


def setup_inputs(seed: int = 0) -> dict:
    keys = jax.random.split(jax.random.key(seed), 7)
    return {
        "image_feats": normal_values(keys[0], (GROUPS, PAIRS, VIS_WIDTH), 1.0, 6.0, ((0, 16), (1, 8))),
        "text_feats": normal_values(keys[1], (GROUPS, PAIRS, TXT_WIDTH), 1.0, 6.0, ((0, 16), (1, 8))),
        "image_head": normal_values(keys[2], (VIS_WIDTH, EMBED), VIS_WIDTH ** -0.5, 0.1875),
        "text_head": normal_values(keys[3], (TXT_WIDTH, EMBED), TXT_WIDTH ** -0.5, 0.21875),
        "image_lse": draw_image_lse(jax.random.fold_in(keys[6], 71), 0),
        "text_lse": draw_text_lse(jax.random.fold_in(keys[6], 71), 0),
    }


logit_scale = 50.0
epsilon = 1e-06

def project_head(feats, weight):
    raw = jnp.dot(feats, weight, preferred_element_type=jnp.float32)
    factor = lax.rsqrt(lax.optimization_barrier(jnp.sum(raw * raw, axis=1, keepdims=True)) + epsilon)
    return (raw * factor, factor)

def pre_gradient(embed, factor, grad):
    inner = lax.optimization_barrier(jnp.sum(embed * grad, axis=1, keepdims=True))
    return (factor * (grad - embed * inner)).astype(jnp.bfloat16)

def group_grads(group):
    image_rows, text_rows, image_head, text_head, lse_img, lse_txt = group
    image_embed, image_scale = project_head(image_rows, image_head)
    text_embed, text_scale = project_head(text_rows, text_head)
    image_round = image_embed.astype(jnp.bfloat16)
    text_round = text_embed.astype(jnp.bfloat16)
    scores = logit_scale * lax.dot_general(image_round, text_round, (((1,), (1,)), ((), ())), preferred_element_type=jnp.float32)
    weights = (0.5 * (jnp.exp(scores - lse_img[:, None]) + jnp.exp(scores - lse_txt[None, :]))).astype(jnp.bfloat16)
    image_sum = jnp.dot(weights, text_round, preferred_element_type=jnp.float32)
    text_sum = lax.dot_general(weights, image_round, (((0,), (0,)), ((), ())), preferred_element_type=jnp.float32)
    image_grad = logit_scale * image_sum - logit_scale * text_round.astype(jnp.float32)
    text_grad = logit_scale * text_sum - logit_scale * image_round.astype(jnp.float32)
    image_pre = pre_gradient(image_embed, image_scale, image_grad)
    text_pre = pre_gradient(text_embed, text_scale, text_grad)
    image_back = lax.dot_general(image_pre, image_head, (((1,), (1,)), ((), ())), preferred_element_type=jnp.float32)
    text_back = lax.dot_general(text_pre, text_head, (((1,), (1,)), ((), ())), preferred_element_type=jnp.float32)
    image_wgrad = lax.dot_general(image_rows, image_pre, (((0,), (0,)), ((), ())), preferred_element_type=jnp.float32)
    text_wgrad = lax.dot_general(text_rows, text_pre, (((0,), (0,)), ((), ())), preferred_element_type=jnp.float32)
    return (image_back, text_back, image_wgrad, text_wgrad)

def reference(image_feats, text_feats, image_head, text_head, image_lse, text_lse):

    def single(index):
        group = (image_feats[index], text_feats[index], image_head, text_head, image_lse[index], text_lse[index])
        return group_grads(group)
    image_back, text_back, image_wgrad, text_wgrad = lax.map(single, jnp.arange(GROUPS, dtype=jnp.int32))
    return (image_back, text_back, lax.optimization_barrier(jnp.sum(image_wgrad, axis=0)), lax.optimization_barrier(jnp.sum(text_wgrad, axis=0)))
```

```python
import functools
import math

import jax
import jax.numpy as jnp
from jax import lax
from jax.experimental import pallas as pl
from jax.experimental.pallas import tpu as pltpu
from jax.sharding import Mesh
from jax.sharding import PartitionSpec as P

BLK = ("y", "xl")
REP = ("z", "xh", "core")
PLANE = ("xl", "z", "xh")

bf16 = jnp.bfloat16
f32 = jnp.float32

logit_scale = 50.0
epsilon = 1e-06
exp2_scale = logit_scale * math.log2(math.e)

ROWS = 512
PAD = 16
EMB = 768
VIS = 1024
TXT = 768
HV = VIS // 2
HT = TXT // 2
HALF = HV + HT


def permute(value, axis, size, shift):
    return lax.ppermute(value, axis, [(i, (i + shift) % size) for i in range(size)])


def nt(a, b):
    return lax.dot_general(a, b, (((1,), (1,)), ((), ())), preferred_element_type=f32)


def tn(a, b):
    return lax.dot_general(a, b, (((0,), (0,)), ((), ())), preferred_element_type=f32)


def nn(a, b):
    return jnp.dot(a, b, preferred_element_type=f32)


def scale_of(raw):
    return lax.rsqrt(jnp.sum(raw * raw, axis=1, keepdims=True) + epsilon)


def pre_gradient(raw, grad):
    factor = scale_of(raw)
    embed = raw * factor
    inner = jnp.sum(embed * grad, axis=1, keepdims=True)
    return (factor * (grad - embed * inner)).astype(bf16)


CH = 256


def tile_kernel(core, i0, i1, t0, t1, t2, t3, hi, ht,
                p1, p2, p3, tbase, ipart, ibase, send, keep,
                zi, ri, ea, zt, rt, eb, w, pre, prei):
    imgs = (i0, i1)
    txts = (t0, t1, t2, t3)
    for b, ref in enumerate(imgs):
        @pl.loop(0, ROWS // CH)
        def _(k, b=b, ref=ref):
            src = pl.ds(pl.multiple_of(k * CH, CH), CH)
            dst = pl.ds(pl.multiple_of(b * ROWS + k * CH, CH), CH)
            raw = nn(ref[src, :], hi[...])
            zi[dst, :] = raw
            ri[dst, :] = (raw * scale_of(raw)).astype(bf16)

        tail = ref[ROWS : ROWS + PAD, :].astype(f32)
        lse = tail[0:1, 0:ROWS] + tail[0:1, ROWS : 2 * ROWS]
        row = 0.5 * jnp.exp(-lse)
        ea[b * ROWS : (b + 1) * ROWS, :] = jnp.broadcast_to(row, (128, ROWS)).T

    for b, ref in enumerate(txts):
        @pl.loop(0, ROWS // CH)
        def _(k, b=b, ref=ref):
            src = pl.ds(pl.multiple_of(k * CH, CH), CH)
            dst = pl.ds(pl.multiple_of(b * ROWS + k * CH, CH), CH)
            raw = nn(ref[src, :], ht[...])
            zt[src, :] = raw
            rt[dst, :] = (raw * scale_of(raw)).astype(bf16)

        tail = ref[ROWS : ROWS + PAD, :].astype(f32)
        lse = tail[0:1, 0:ROWS] + tail[1:2, 0:ROWS]
        eb[...] = jnp.broadcast_to(0.5 * jnp.exp(-lse), (8, ROWS))

        @pl.loop(0, 2 * ROWS // CH)
        def _(k, b=b):
            rows = pl.ds(pl.multiple_of(k * CH, CH), CH)
            s = nt(ri[rows, :], rt[b * ROWS : (b + 1) * ROWS, :])
            col = ea[rows, :]
            both = jnp.concatenate([col] * (ROWS // 128), axis=1) + eb[0:1, :]
            w[rows, b * ROWS : (b + 1) * ROWS] = (jnp.exp2(s * exp2_scale) * both).astype(bf16)

        @pl.loop(0, ROWS // CH)
        def _(k, b=b):
            src = pl.ds(pl.multiple_of(k * CH, CH), CH)
            dst = pl.ds(pl.multiple_of(b * ROWS + k * CH, CH), CH)
            g = tn(w[:, pl.ds(pl.multiple_of(b * ROWS + k * CH, CH), CH)], ri[...])
            if b == 0:
                g = g - ri[src, :].astype(f32)
                tbase[src, :] = g
            else:
                (p1, p2, p3)[b - 1][src, :] = g.astype(bf16)
            pre[dst, :] = pre_gradient(zt[src, :], logit_scale * g)

    for b in range(2):
        @pl.loop(0, ROWS // CH)
        def _(k, b=b):
            src = pl.ds(pl.multiple_of(k * CH, CH), CH)
            dst = pl.ds(pl.multiple_of(b * ROWS + k * CH, CH), CH)
            g = nn(w[dst, :], rt[...])
            if b == 0:
                g = g - rt[src, :].astype(f32)
                ibase[src, :] = g
            else:
                ipart[src, :] = g.astype(bf16)
            prei[dst, :] = pre_gradient(zi[dst, :], logit_scale * g)

    mine = core[0]

    def head_half(which, store):
        ci = pl.ds(pl.multiple_of(which * HV, 128), HV)
        ct = pl.ds(pl.multiple_of(which * HT, 128), HT)
        total = None
        for b, ref in enumerate(imgs):
            part = tn(ref[0:ROWS, ci], prei[b * ROWS : (b + 1) * ROWS, :])
            total = part if total is None else total + part
        store(0, HV, total)
        total = None
        for b, ref in enumerate(txts):
            part = tn(ref[0:ROWS, ct], pre[b * ROWS : (b + 1) * ROWS, :])
            total = part if total is None else total + part
        store(HV, HT, total)

    def store_send(at, n, value):
        send[at : at + n, :] = value.astype(bf16)

    def store_keep(at, n, value):
        keep[at : at + n, :] = value

    head_half(1 - mine, store_send)
    head_half(mine, store_keep)


VMEM = pl.BlockSpec(memory_space=pltpu.VMEM)
SMEM = pl.BlockSpec(memory_space=pltpu.SMEM)


def tile_call(core, i0, i1, texts, image_head, text_head):
    block = jax.ShapeDtypeStruct((ROWS, EMB), bf16)
    wide = jax.ShapeDtypeStruct((ROWS, EMB), f32)
    return pl.pallas_call(
        tile_kernel,
        out_shape=(block, block, block, wide, block, wide,
                   jax.ShapeDtypeStruct((HALF, EMB), bf16), jax.ShapeDtypeStruct((HALF, EMB), f32)),
        in_specs=[SMEM] + [VMEM] * 8,
        out_specs=(VMEM,) * 8,
        scratch_shapes=[
            pltpu.VMEM((2 * ROWS, EMB), f32),
            pltpu.VMEM((2 * ROWS, EMB), bf16),
            pltpu.VMEM((2 * ROWS, 128), f32),
            pltpu.VMEM((ROWS, EMB), f32),
            pltpu.VMEM((4 * ROWS, EMB), bf16),
            pltpu.VMEM((8, ROWS), f32),
            pltpu.VMEM((2 * ROWS, 4 * ROWS), bf16),
            pltpu.VMEM((4 * ROWS, EMB), bf16),
            pltpu.VMEM((2 * ROWS, EMB), bf16),
        ],
        compiler_params=pltpu.CompilerParams(vmem_limit_bytes=56 * 1024 * 1024),
        cost_estimate=pl.CostEstimate(flops=20 * 10**9, bytes_accessed=20 * 10**6, transcendentals=2 * 10**6),
        name="tile",
    )(core, i0, i1, *texts, image_head, text_head)


def back_kernel(n, feats, head, base, *rest):
    parts, out = rest[:n], rest[n]

    @pl.loop(0, ROWS // CH)
    def _(k):
        rows = pl.ds(pl.multiple_of(k * CH, CH), CH)
        raw = nn(feats[rows, :], head[...])
        g = base[rows, :]
        for p in parts:
            g = g + p[rows, :].astype(f32)
        out[rows, :] = nt(pre_gradient(raw, logit_scale * g), head[...])


def back_call(feats, head, base, parts):
    width = head.shape[0]
    return pl.pallas_call(
        functools.partial(back_kernel, len(parts)),
        out_shape=jax.ShapeDtypeStruct((ROWS, width), f32),
        in_specs=[VMEM] * (3 + len(parts)),
        out_specs=VMEM,
        compiler_params=pltpu.CompilerParams(vmem_limit_bytes=40 * 1024 * 1024),
        cost_estimate=pl.CostEstimate(flops=4 * ROWS * EMB * width, bytes_accessed=10 * 10**6, transcendentals=0),
        name="back",
    )(feats, head, base, *parts)


def final_kernel(core, own, other, image, text):
    mine = core[0]
    for ref, which in ((own, mine), (other, 1 - mine)):
        image[pl.ds(pl.multiple_of(which * HV, 128), HV), :] = ref[0:HV, :].astype(f32)
        text[pl.ds(pl.multiple_of(which * HT, 128), HT), :] = ref[HV:HALF, :].astype(f32)


def final_call(core, own, other):
    return pl.pallas_call(
        final_kernel,
        out_shape=(jax.ShapeDtypeStruct((VIS, EMB), f32), jax.ShapeDtypeStruct((TXT, EMB), f32)),
        in_specs=[SMEM, VMEM, VMEM],
        out_specs=(VMEM, VMEM),
        compiler_params=pltpu.CompilerParams(vmem_limit_bytes=40 * 1024 * 1024),
        name="final",
    )(core, own, other)


def split_lse(lse):
    high = lse.astype(bf16)
    low = (lse - high.astype(f32)).astype(bf16)
    return high, low


def reduce_heads(send, keep):
    part = keep + permute(send, "core", 2, 1).astype(f32)
    part = part.astype(bf16).reshape(16, HALF // 16, EMB)
    part = lax.all_to_all(part, PLANE, 0, 0, tiled=True)
    part = jnp.sum(part.astype(f32), axis=0).astype(bf16)
    others = [permute(part, "y", 4, d).astype(f32) for d in (1, 3, 2)]
    part = ((part.astype(f32) + others[2]) + (others[0] + others[1])).astype(bf16)
    whole = jnp.broadcast_to(part[None], (16, HALF // 16, EMB))
    whole = lax.all_to_all(whole, PLANE, 0, 0, tiled=True).reshape(HALF, EMB)
    return whole, permute(whole, "core", 2, 1)


def shards(image_feats, text_feats, image_head, text_head, image_lse, text_lse):
    image_rows = image_feats[0]
    text_rows = text_feats[0]
    core = lax.axis_index("core").astype(jnp.int32).reshape(1)

    high, low = split_lse(text_lse)
    text_msg = jnp.concatenate(
        [text_rows, jnp.pad(jnp.concatenate([high, low], axis=0), ((0, PAD - 2), (0, TXT - ROWS)))], axis=0
    )
    high, low = split_lse(image_lse)
    image_msg = jnp.concatenate(
        [image_rows, jnp.pad(jnp.concatenate([high, low], axis=1), ((0, PAD - 1), (0, 0)))], axis=0
    )
    texts = [text_msg] + [permute(text_msg, "y", 4, d) for d in (1, 3, 2)]
    partner = permute(image_msg, "xl", 2, 1)

    p1, p2, p3, tbase, ipart, ibase, send, keep = tile_call(core, image_msg, partner, texts, image_head, text_head)

    own, other = reduce_heads(send, keep)
    text_parts = [permute(p, "y", 4, -d) for p, d in ((p1, 1), (p2, 3), (p3, 2))]
    image_part = permute(ipart, "xl", 2, 1)
    text_back = back_call(text_rows, text_head, tbase, text_parts)
    image_back = back_call(image_rows, image_head, ibase, [image_part])
    image_total, text_total = final_call(core, own, other)
    return (image_back[None], text_back[None], image_total, text_total)


def solution(mesh):
    finer = Mesh(mesh.devices.reshape(4, 2, 4, 2, 2), BLK + REP)
    return jax.shard_map(
        shards,
        mesh=finer,
        in_specs=(P(REP, BLK, None), P(REP, BLK, None), P(), P(), P(REP, BLK), P(REP, BLK)),
        out_specs=(P(REP, BLK, None), P(REP, BLK, None), P(), P()),
        check_vma=False,
    )
```

```python
import functools
import math

import jax
import jax.numpy as jnp
from jax import lax
from jax.experimental import pallas as pl
from jax.experimental.pallas import tpu as pltpu
from jax.sharding import Mesh
from jax.sharding import PartitionSpec as P

BLK = ("y", "xl")
REP = ("z", "xh", "core")
PLANE = ("xl", "z", "xh")

bf16 = jnp.bfloat16
f32 = jnp.float32

logit_scale = 50.0
epsilon = 1e-06
exp2_scale = logit_scale * math.log2(math.e)

ROWS = 512
PAD = 16
EMB = 768
VIS = 1024
TXT = 768
HV = VIS // 2
HT = TXT // 2
HALF = HV + HT


def permute(value, axis, size, shift):
    return lax.ppermute(value, axis, [(i, (i + shift) % size) for i in range(size)])


def nt(a, b):
    return lax.dot_general(a, b, (((1,), (1,)), ((), ())), preferred_element_type=f32)


def tn(a, b):
    return lax.dot_general(a, b, (((0,), (0,)), ((), ())), preferred_element_type=f32)


def nn(a, b):
    return jnp.dot(a, b, preferred_element_type=f32)


def scale_of(raw):
    return lax.rsqrt(jnp.sum(raw * raw, axis=1, keepdims=True) + epsilon)


def pre_gradient(raw, grad):
    factor = scale_of(raw)
    embed = raw * factor
    inner = jnp.sum(embed * grad, axis=1, keepdims=True)
    return (factor * (grad - embed * inner)).astype(bf16)


CH = 256
MID = ROWS // 2
CHUNKS = range(0, ROWS, CH)
ANY = pl.BlockSpec(memory_space=pl.ANY)
VMEM = pl.BlockSpec(memory_space=pltpu.VMEM)
SMEM = pl.BlockSpec(memory_space=pltpu.SMEM)
LIMIT = pltpu.CompilerParams(vmem_limit_bytes=48 * 1024 * 1024)


def wide(rows, columns=EMB):
    return jax.ShapeDtypeStruct((rows, columns), f32)


def narrow(rows, columns=EMB):
    return jax.ShapeDtypeStruct((rows, columns), bf16)


class Copies:
    def __init__(self, sems):
        self.sems = sems
        self.count = 0

    def start(self, src, dst):
        copy = pltpu.make_async_copy(src, dst, self.sems.at[self.count])
        self.count += 1
        copy.start()
        return copy


def own_kernel(image, text, hi, ht, zi, ri, zt, rt):
    for feats, head, raw_ref, round_ref in ((image, hi, zi, ri), (text, ht, zt, rt)):
        for c in CHUNKS:
            raw = nn(feats[c : c + CH, :], head[...])
            raw_ref[c : c + CH, :] = raw
            round_ref[c : c + CH, :] = (raw * scale_of(raw)).astype(bf16)


def own_call(image, text, hi, ht):
    return pl.pallas_call(
        own_kernel,
        out_shape=(wide(ROWS), narrow(ROWS), wide(ROWS), narrow(ROWS)),
        in_specs=[VMEM] * 4,
        out_specs=(VMEM,) * 4,
        compiler_params=LIMIT,
        cost_estimate=pl.CostEstimate(flops=14 * 10**8, bytes_accessed=10**7, transcendentals=0),
        name="own",
    )(image, text, hi, ht)


def column_weights(lse_row):
    row = 0.5 * jnp.exp(-lse_row)
    return jnp.broadcast_to(row, (128, ROWS)).T


def image_tail(tail):
    tail = tail[...].astype(f32)
    return tail[0:1, 0:ROWS] + tail[0:1, ROWS : 2 * ROWS]


def text_tail(tail):
    tail = tail[...].astype(f32)
    return tail[0:1, 0:ROWS] + tail[1:2, 0:ROWS]


def fill_weights(ri, rt_block, ea, lse_row, w, column):
    eb = 0.5 * jnp.exp(-lse_row)
    for r in range(0, 2 * ROWS, CH):
        s = nt(ri[r : r + CH, :], rt_block)
        both = jnp.concatenate([ea[r : r + CH, :]] * (ROWS // 128), axis=1) + eb
        w[r : r + CH, column : column + ROWS] = (jnp.exp2(s * exp2_scale) * both).astype(bf16)


def first_kernel(i1, t0, t1, t2, ri0, rt0, zt0, lse_i, lse_t, hi, ht,
                 tbase, p1, p2, ri1, zi1, ig, wt,
                 ri, ea, t, rt, zt, w, pre, image, head_i, head_t, itail, ttail, zout, bout, pout, iout, wout, sems):
    io = Copies(sems)
    n = ROWS
    c_image = io.start(i1.at[pl.ds(0, n)], image)
    c_hi = io.start(hi, head_i)
    c_itail = io.start(i1.at[pl.ds(n, PAD)], itail)
    c_rt0 = io.start(rt0, rt.at[pl.ds(0, n)])
    c_ri0 = io.start(ri0, ri.at[pl.ds(0, n)])
    c_zt0 = io.start(zt0, zt.at[pl.ds(0, n)])
    c_t = [io.start(t0, t.at[pl.ds(0, n)])]
    c_ht = io.start(ht, head_t)
    c_tail = []
    for b, ref in ((1, t1), (2, t2)):
        c_t.append(io.start(ref.at[pl.ds(0, n)], t.at[pl.ds(b * n, n)]))
        c_tail.append(io.start(ref.at[pl.ds(n, PAD)], ttail.at[b - 1]))
    outs = []

    c_image.wait()
    c_hi.wait()
    for c in CHUNKS:
        raw = nn(image[c : c + CH, :], head_i[...])
        zout[c : c + CH, :] = raw
        ri[n + c : n + c + CH, :] = (raw * scale_of(raw)).astype(bf16)
    outs.append(io.start(zout, zi1))
    outs.append(io.start(ri.at[pl.ds(n, n)], ri1))
    c_itail.wait()
    ea[0:n, :] = column_weights(lse_i[...])
    ea[n : 2 * n, :] = column_weights(image_tail(itail))
    c_rt0.wait()
    c_ri0.wait()
    for b in range(3):
        at = b * n
        c_t[b].wait()
        if b == 0:
            c_zt0.wait()
            lse_row = lse_t[...]
        else:
            c_tail[b - 1].wait()
            if b == 1:
                c_ht.wait()
            for c in CHUNKS:
                raw = nn(t[at + c : at + c + CH, :], head_t[...])
                zt[at + c : at + c + CH, :] = raw
                rt[at + c : at + c + CH, :] = (raw * scale_of(raw)).astype(bf16)
            lse_row = text_tail(ttail.at[b - 1])
        fill_weights(ri, rt[at : at + n, :], ea, lse_row, w, at)
        for c in CHUNKS:
            g = tn(w[:, at + c : at + c + CH], ri[...])
            if b == 0:
                g = g - ri[c : c + CH, :].astype(f32)
                bout[c : c + CH, :] = g
            else:
                pout[b - 1, c : c + CH, :] = g.astype(bf16)
            pre[at + c : at + c + CH, :] = pre_gradient(zt[at + c : at + c + CH, :], logit_scale * g)
        outs.append(io.start(bout, tbase) if b == 0 else io.start(pout.at[b - 1], (p1, p2)[b - 1]))
    for r in range(0, 2 * n, CH):
        g = nn(w[r : r + CH, :], rt[...])
        if r < n:
            g = g - rt[r : r + CH, :].astype(f32)
        iout[r : r + CH, :] = g
    outs.append(io.start(iout, ig))
    for r in range(0, TXT, CH):
        wout[r : r + CH, :] = tn(t[:, r : r + CH], pre[...])
    outs.append(io.start(wout, wt))
    for copy in outs:
        copy.wait()


def first_call(i1, t0, t1, t2, ri0, rt0, zt0, lse_i, lse_t, hi, ht):
    n = ROWS
    return pl.pallas_call(
        first_kernel,
        out_shape=(wide(n), narrow(n), narrow(n), narrow(n), wide(n), wide(2 * n), wide(TXT)),
        in_specs=[ANY] * 7 + [VMEM] * 2 + [ANY] * 2,
        out_specs=(ANY,) * 7,
        scratch_shapes=[
            pltpu.VMEM((2 * n, EMB), bf16),
            pltpu.VMEM((2 * n, 128), f32),
            pltpu.VMEM((3 * n, TXT), bf16),
            pltpu.VMEM((3 * n, EMB), bf16),
            pltpu.VMEM((3 * n, EMB), f32),
            pltpu.VMEM((2 * n, 3 * n), bf16),
            pltpu.VMEM((3 * n, EMB), bf16),
            pltpu.VMEM((n, VIS), bf16),
            pltpu.VMEM((VIS, EMB), bf16),
            pltpu.VMEM((TXT, EMB), bf16),
            pltpu.VMEM((PAD, VIS), bf16),
            pltpu.VMEM((2, PAD, TXT), bf16),
            pltpu.VMEM((n, EMB), f32),
            pltpu.VMEM((n, EMB), f32),
            pltpu.VMEM((2, n, EMB), bf16),
            pltpu.VMEM((2 * n, EMB), f32),
            pltpu.VMEM((TXT, EMB), f32),
            pltpu.SemaphoreType.DMA((24,)),
        ],
        compiler_params=LIMIT,
        cost_estimate=pl.CostEstimate(flops=12 * 10**9, bytes_accessed=20 * 10**6, transcendentals=2 * 10**6),
        name="first",
    )(i1, t0, t1, t2, ri0, rt0, zt0, lse_i, lse_t, hi, ht)


def second_kernel(core, i0, i1, t3a, t3b, p1, p2, ri0, ri1, zi0, zi1, ig, wt, lse_i, ht,
                  up, down, ipart, ibase, send, keep,
                  ri, ea, t, rt, zt, w, pre, prei, image, head_t, itail, ttail, zi, gi, wsum,
                  pout, qout, bout, sout, kout, sems):
    io = Copies(sems)
    n = ROWS
    c_t = [io.start(t3a, t.at[pl.ds(0, MID)]), io.start(t3b.at[pl.ds(0, n - MID)], t.at[pl.ds(MID, n - MID)])]
    c_ht = io.start(ht, head_t)
    c_ttail = io.start(t3b.at[pl.ds(n - MID, PAD)], ttail)
    c_itail = io.start(i1.at[pl.ds(n, PAD)], itail)
    c_ri = [io.start(ri0, ri.at[pl.ds(0, n)]), io.start(ri1, ri.at[pl.ds(n, n)])]
    c_ig = io.start(ig, gi)
    c_zi = [io.start(zi0, zi.at[pl.ds(0, n)]), io.start(zi1, zi.at[pl.ds(n, n)])]
    c_image = [io.start(i0, image.at[pl.ds(0, n)]), io.start(i1.at[pl.ds(0, n)], image.at[pl.ds(n, n)])]
    c_wt = io.start(wt, wsum)
    outs = [io.start(p2, up.at[pl.ds(0, n)]), io.start(p1, down.at[pl.ds(0, n)])]

    c_itail.wait()
    ea[0:n, :] = column_weights(lse_i[...])
    ea[n : 2 * n, :] = column_weights(image_tail(itail))
    for copy in c_t:
        copy.wait()
    c_ht.wait()
    for c in CHUNKS:
        raw = nn(t[c : c + CH, :], head_t[...])
        zt[c : c + CH, :] = raw
        rt[c : c + CH, :] = (raw * scale_of(raw)).astype(bf16)
    c_ttail.wait()
    for copy in c_ri:
        copy.wait()
    fill_weights(ri, rt[...], ea, text_tail(ttail), w, 0)
    for c in CHUNKS:
        g = tn(w[:, c : c + CH], ri[...])
        pout[c : c + CH, :] = g.astype(bf16)
        pre[c : c + CH, :] = pre_gradient(zt[c : c + CH, :], logit_scale * g)
    outs.append(io.start(pout.at[pl.ds(0, MID)], up.at[pl.ds(n, MID)]))
    outs.append(io.start(pout.at[pl.ds(MID, n - MID)], down.at[pl.ds(n, n - MID)]))
    c_ig.wait()
    for copy in c_zi:
        copy.wait()
    for r in range(0, 2 * n, CH):
        g = gi[r : r + CH, :] + nn(w[r : r + CH, :], rt[...])
        if r < n:
            bout[r : r + CH, :] = g
        else:
            qout[r - n : r - n + CH, :] = g.astype(bf16)
        prei[r : r + CH, :] = pre_gradient(zi[r : r + CH, :], logit_scale * g)
    outs.append(io.start(bout, ibase))
    outs.append(io.start(qout, ipart))
    for copy in c_image:
        copy.wait()
    c_wt.wait()
    mine = core[0]
    for which, ref, out in ((1 - mine, sout, send), (mine, kout, keep)):
        for c in range(0, HV, CH):
            cols = pl.ds(pl.multiple_of(which * HV + c, 128), CH)
            ref[c : c + CH, :] = tn(image[:, cols], prei[...]).astype(ref.dtype)
        for c in range(0, HT, 128):
            cols = pl.ds(pl.multiple_of(which * HT + c, 128), 128)
            ref[HV + c : HV + c + 128, :] = (wsum[cols, :] + tn(t[:, cols], pre[...])).astype(ref.dtype)
        outs.append(io.start(ref, out))
    for copy in outs:
        copy.wait()


def second_call(core, i0, i1, t3a, t3b, p1, p2, ri0, ri1, zi0, zi1, ig, wt, lse_i, ht):
    n = ROWS
    return pl.pallas_call(
        second_kernel,
        out_shape=(narrow(n + MID), narrow(n + MID), narrow(n), wide(n), narrow(HALF), wide(HALF)),
        in_specs=[SMEM] + [ANY] * 12 + [VMEM] + [ANY],
        out_specs=(ANY,) * 6,
        scratch_shapes=[
            pltpu.VMEM((2 * n, EMB), bf16),
            pltpu.VMEM((2 * n, 128), f32),
            pltpu.VMEM((n, TXT), bf16),
            pltpu.VMEM((n, EMB), bf16),
            pltpu.VMEM((n, EMB), f32),
            pltpu.VMEM((2 * n, n), bf16),
            pltpu.VMEM((n, EMB), bf16),
            pltpu.VMEM((2 * n, EMB), bf16),
            pltpu.VMEM((2 * n, VIS), bf16),
            pltpu.VMEM((TXT, EMB), bf16),
            pltpu.VMEM((PAD, VIS), bf16),
            pltpu.VMEM((PAD, TXT), bf16),
            pltpu.VMEM((2 * n, EMB), f32),
            pltpu.VMEM((2 * n, EMB), f32),
            pltpu.VMEM((TXT, EMB), f32),
            pltpu.VMEM((n, EMB), bf16),
            pltpu.VMEM((n, EMB), bf16),
            pltpu.VMEM((n, EMB), f32),
            pltpu.VMEM((HALF, EMB), bf16),
            pltpu.VMEM((HALF, EMB), f32),
            pltpu.SemaphoreType.DMA((24,)),
        ],
        compiler_params=LIMIT,
        cost_estimate=pl.CostEstimate(flops=8 * 10**9, bytes_accessed=20 * 10**6, transcendentals=10**6),
        name="second",
    )(core, i0, i1, t3a, t3b, p1, p2, ri0, ri1, zi0, zi1, ig, wt, lse_i, ht)


def back_kernel(whole, split, raw, head, base, *rest):
    out = rest[-1]
    for i, c in enumerate(CHUNKS):
        g = base[c : c + CH, :]
        for p in rest[:whole]:
            g = g + p[c : c + CH, :].astype(f32)
        if split:
            g = g + rest[whole + i][...].astype(f32)
        out[c : c + CH, :] = nt(pre_gradient(raw[c : c + CH, :], logit_scale * g), head[...])


def back_call(raw, head, base, parts, halves=()):
    width = head.shape[0]
    return pl.pallas_call(
        functools.partial(back_kernel, len(parts), len(halves) > 0),
        out_shape=wide(ROWS, width),
        in_specs=[VMEM] * (3 + len(parts) + len(halves)),
        out_specs=VMEM,
        compiler_params=pltpu.CompilerParams(vmem_limit_bytes=40 * 1024 * 1024),
        cost_estimate=pl.CostEstimate(flops=2 * ROWS * EMB * width, bytes_accessed=10 * 10**6, transcendentals=0),
        name="back",
    )(raw, head, base, *parts, *halves)


def final_kernel(core, own, other, image, text):
    mine = core[0]
    for ref, which in ((own, mine), (other, 1 - mine)):
        image[pl.ds(pl.multiple_of(which * HV, 128), HV), :] = ref[0:HV, :].astype(f32)
        text[pl.ds(pl.multiple_of(which * HT, 128), HT), :] = ref[HV:HALF, :].astype(f32)


def final_call(core, own, other):
    return pl.pallas_call(
        final_kernel,
        out_shape=(jax.ShapeDtypeStruct((VIS, EMB), f32), jax.ShapeDtypeStruct((TXT, EMB), f32)),
        in_specs=[SMEM, VMEM, VMEM],
        out_specs=(VMEM, VMEM),
        compiler_params=pltpu.CompilerParams(vmem_limit_bytes=40 * 1024 * 1024),
        name="final",
    )(core, own, other)


def split_lse(lse):
    high = lse.astype(bf16)
    low = (lse - high.astype(f32)).astype(bf16)
    return high, low


def reduce_heads(send, keep):
    part = keep + permute(send, "core", 2, 1).astype(f32)
    part = part.astype(bf16).reshape(16, HALF // 16, EMB)
    part = lax.all_to_all(part, PLANE, 0, 0, tiled=True)
    return jnp.sum(part.astype(f32), axis=0).astype(bf16)


def spread_heads(part):
    others = [permute(part, "y", 4, d).astype(f32) for d in (1, 3, 2)]
    part = ((part.astype(f32) + others[2]) + (others[0] + others[1])).astype(bf16)
    whole = jnp.broadcast_to(part[None], (16, HALF // 16, EMB))
    return lax.all_to_all(whole, PLANE, 0, 0, tiled=True).reshape(HALF, EMB)


def shards(image_feats, text_feats, image_head, text_head, image_lse, text_lse):
    image_rows = image_feats[0]
    text_rows = text_feats[0]
    core = lax.axis_index("core").astype(jnp.int32).reshape(1)

    high, low = split_lse(text_lse)
    text_msg = jnp.concatenate(
        [text_rows, jnp.pad(jnp.concatenate([high, low], axis=0), ((0, PAD - 2), (0, TXT - ROWS)))], axis=0
    )
    high, low = split_lse(image_lse)
    image_msg = jnp.concatenate(
        [image_rows, jnp.pad(jnp.concatenate([high, low], axis=1), ((0, PAD - 1), (0, 0)))], axis=0
    )
    t1 = permute(text_msg, "y", 4, 1)
    t2 = permute(text_msg, "y", 4, 3)
    i1 = permute(image_msg, "xl", 2, 1)
    zi0, ri0, zt0, rt0 = own_call(image_rows, text_rows, image_head, text_head)
    t3a = permute(t1[:MID], "y", 4, 1)
    t3b = permute(t2[MID:], "y", 4, 3)

    tbase, p1, p2, ri1, zi1, ig, wt = first_call(
        i1, text_rows, t1, t2, ri0, rt0, zt0, image_lse, text_lse, image_head, text_head
    )
    up, down, ipart, ibase, send, keep = second_call(
        core, image_rows, i1, t3a, t3b, p1, p2, ri0, ri1, zi0, zi1, ig, wt, image_lse, text_head
    )
    part = reduce_heads(send, keep)
    up, down, ipart = permute(up, "y", 4, 1), permute(down, "y", 4, 3), permute(ipart, "xl", 2, 1)
    part, up, down, ipart = lax.optimization_barrier((part, up, down, ipart))
    whole = spread_heads(part)
    top, bottom = permute(up[ROWS:], "y", 4, 1), permute(down[ROWS:], "y", 4, 3)
    text_back = back_call(zt0, text_head, tbase, [up, down], [top, bottom])
    image_back = back_call(zi0, image_head, ibase, [ipart])
    whole, text_back, image_back = lax.optimization_barrier((whole, text_back, image_back))
    image_total, text_total = final_call(core, whole, permute(whole, "core", 2, 1))
    return (image_back[None], text_back[None], image_total, text_total)


def solution(mesh):
    finer = Mesh(mesh.devices.reshape(4, 2, 4, 2, 2), BLK + REP)
    return jax.shard_map(
        shards,
        mesh=finer,
        in_specs=(P(REP, BLK, None), P(REP, BLK, None), P(), P(), P(REP, BLK), P(REP, BLK)),
        out_specs=(P(REP, BLK, None), P(REP, BLK, None), P(), P()),
        check_vma=False,
    )
```

```python
import functools
import math

import jax
import jax.numpy as jnp
from jax import lax
from jax.experimental import pallas as pl
from jax.experimental.pallas import tpu as pltpu
from jax.sharding import Mesh
from jax.sharding import PartitionSpec as P

BLK = ("y", "xl")
REP = ("z", "xh", "core")
PLANE = ("xl", "z", "xh")

bf16 = jnp.bfloat16
f32 = jnp.float32

logit_scale = 50.0
epsilon = 1e-06
exp2_scale = logit_scale * math.log2(math.e)

ROWS = 512
PAD = 16
EMB = 768
VIS = 1024
TXT = 768
HV = VIS // 2
HT = TXT // 2
HALF = HV + HT


def permute(value, axis, size, shift):
    return lax.ppermute(value, axis, [(i, (i + shift) % size) for i in range(size)])


def nt(a, b):
    return lax.dot_general(a, b, (((1,), (1,)), ((), ())), preferred_element_type=f32)


def tn(a, b):
    return lax.dot_general(a, b, (((0,), (0,)), ((), ())), preferred_element_type=f32)


def nn(a, b):
    return jnp.dot(a, b, preferred_element_type=f32)


def scale_of(raw):
    return lax.rsqrt(jnp.sum(raw * raw, axis=1, keepdims=True) + epsilon)


def pre_gradient(raw, grad):
    factor = scale_of(raw)
    embed = raw * factor
    inner = jnp.sum(embed * grad, axis=1, keepdims=True)
    return (factor * (grad - embed * inner)).astype(bf16)


CH = 256
MID = ROWS // 2
CHUNKS = range(0, ROWS, CH)
ANY = pl.BlockSpec(memory_space=pl.ANY)
VMEM = pl.BlockSpec(memory_space=pltpu.VMEM)
SMEM = pl.BlockSpec(memory_space=pltpu.SMEM)
LIMIT = pltpu.CompilerParams(vmem_limit_bytes=48 * 1024 * 1024)
MOST = pltpu.CompilerParams(vmem_limit_bytes=60 * 1024 * 1024)


def wide(rows, columns=EMB):
    return jax.ShapeDtypeStruct((rows, columns), f32)


def narrow(rows, columns=EMB):
    return jax.ShapeDtypeStruct((rows, columns), bf16)


class Copies:
    def __init__(self, sems):
        self.sems = sems
        self.count = 0

    def start(self, src, dst):
        copy = pltpu.make_async_copy(src, dst, self.sems.at[self.count])
        self.count += 1
        copy.start()
        return copy


def pack_kernel(text, image, lse_t, lse_i, text_a, text_b, image_msg):
    n = ROWS
    text_a[...] = text[0:MID, :]
    text_b[0 : n - MID, :] = text[MID:n, :]
    row = lax.broadcasted_iota(jnp.int32, (PAD, n), 0)
    high = lse_t[...].astype(bf16).astype(f32)
    text_b[n - MID :, 0:n] = jnp.where(row == 0, high, lse_t[...] - high).astype(bf16)
    text_b[n - MID :, n:TXT] = jnp.zeros((PAD, TXT - n), bf16)
    image_msg[0:n, :] = image[...]
    high = lse_i[...].astype(bf16).astype(f32)
    image_msg[n:, 0:n] = jnp.broadcast_to(high, (PAD, n)).astype(bf16)
    image_msg[n:, n : 2 * n] = jnp.broadcast_to(lse_i[...] - high, (PAD, n)).astype(bf16)


def pack_call(text, image, lse_t, lse_i):
    return pl.pallas_call(
        pack_kernel,
        out_shape=(narrow(MID, TXT), narrow(ROWS - MID + PAD, TXT), narrow(ROWS + PAD, VIS)),
        in_specs=[VMEM] * 4,
        out_specs=(VMEM,) * 3,
        compiler_params=MOST,
        cost_estimate=pl.CostEstimate(flops=10**5, bytes_accessed=4 * 10**6, transcendentals=0),
        name="pack",
    )(text, image, lse_t, lse_i)


def own_kernel(image, text, hi, ht, zi, ri, zt, rt):
    for feats, head, raw_ref, round_ref in ((image, hi, zi, ri), (text, ht, zt, rt)):
        for c in CHUNKS:
            raw = nn(feats[c : c + CH, :], head[...])
            raw_ref[c : c + CH, :] = raw
            round_ref[c : c + CH, :] = (raw * scale_of(raw)).astype(bf16)


def own_call(image, text, hi, ht):
    return pl.pallas_call(
        own_kernel,
        out_shape=(wide(ROWS), narrow(ROWS), wide(ROWS), narrow(ROWS)),
        in_specs=[VMEM] * 4,
        out_specs=(VMEM,) * 4,
        compiler_params=MOST,
        cost_estimate=pl.CostEstimate(flops=14 * 10**8, bytes_accessed=10**7, transcendentals=0),
        name="own",
    )(image, text, hi, ht)


def column_weights(lse_row):
    row = 0.5 * jnp.exp(-lse_row)
    return jnp.broadcast_to(row, (128, ROWS)).T


def image_tail(tail):
    tail = tail[...].astype(f32)
    return tail[0:1, 0:ROWS] + tail[0:1, ROWS : 2 * ROWS]


def text_tail(tail):
    tail = tail[...].astype(f32)
    return tail[0:1, 0:ROWS] + tail[1:2, 0:ROWS]


def fill_weights(ri, rt_block, ea, lse_row, w, column):
    eb = 0.5 * jnp.exp(-lse_row)
    for r in range(0, 2 * ROWS, CH):
        s = nt(ri[r : r + CH, :], rt_block)
        both = jnp.concatenate([ea[r : r + CH, :]] * (ROWS // 128), axis=1) + eb
        w[r : r + CH, column : column + ROWS] = (jnp.exp2(s * exp2_scale) * both).astype(bf16)


def first_kernel(i1, t0, t1a, t1b, t2a, t2b, ri0, rt0, zt0, lse_i, lse_t, hi, ht,
                 tbase, p1, p2, ri1, zi1, ig, wt,
                 ri, ea, t, rt, zt, w, pre, image, head_i, head_t, itail, ttail, zout, bout, pout, iout, wout, sems):
    io = Copies(sems)
    n = ROWS
    c_image = io.start(i1.at[pl.ds(0, n)], image)
    c_hi = io.start(hi, head_i)
    c_itail = io.start(i1.at[pl.ds(n, PAD)], itail)
    c_rt0 = io.start(rt0, rt.at[pl.ds(0, n)])
    c_ri0 = io.start(ri0, ri.at[pl.ds(0, n)])
    c_zt0 = io.start(zt0, zt.at[pl.ds(0, n)])
    c_t = [[io.start(t0, t.at[pl.ds(0, n)])]]
    c_ht = io.start(ht, head_t)
    c_tail = []
    for b, top, low in ((1, t1a, t1b), (2, t2a, t2b)):
        c_t.append([
            io.start(top, t.at[pl.ds(b * n, MID)]),
            io.start(low.at[pl.ds(0, n - MID)], t.at[pl.ds(b * n + MID, n - MID)]),
        ])
        c_tail.append(io.start(low.at[pl.ds(n - MID, PAD)], ttail.at[b - 1]))
    outs = []

    c_image.wait()
    c_hi.wait()
    for c in CHUNKS:
        raw = nn(image[c : c + CH, :], head_i[...])
        zout[c : c + CH, :] = raw
        ri[n + c : n + c + CH, :] = (raw * scale_of(raw)).astype(bf16)
    outs.append(io.start(zout, zi1))
    outs.append(io.start(ri.at[pl.ds(n, n)], ri1))
    c_itail.wait()
    ea[0:n, :] = column_weights(lse_i[...])
    ea[n : 2 * n, :] = column_weights(image_tail(itail))
    c_rt0.wait()
    c_ri0.wait()
    for b in range(3):
        at = b * n
        for copy in c_t[b]:
            copy.wait()
        if b == 0:
            c_zt0.wait()
            lse_row = lse_t[...]
        else:
            c_tail[b - 1].wait()
            if b == 1:
                c_ht.wait()
            for c in CHUNKS:
                raw = nn(t[at + c : at + c + CH, :], head_t[...])
                zt[at + c : at + c + CH, :] = raw
                rt[at + c : at + c + CH, :] = (raw * scale_of(raw)).astype(bf16)
            lse_row = text_tail(ttail.at[b - 1])
        fill_weights(ri, rt[at : at + n, :], ea, lse_row, w, at)
        for c in CHUNKS:
            g = tn(w[:, at + c : at + c + CH], ri[...])
            if b == 0:
                g = g - ri[c : c + CH, :].astype(f32)
                bout[c : c + CH, :] = g
            else:
                pout[b - 1, c : c + CH, :] = g.astype(bf16)
            pre[at + c : at + c + CH, :] = pre_gradient(zt[at + c : at + c + CH, :], logit_scale * g)
        outs.append(io.start(bout, tbase) if b == 0 else io.start(pout.at[b - 1], (p1, p2)[b - 1]))
    for r in range(0, 2 * n, CH):
        g = nn(w[r : r + CH, :], rt[...])
        if r < n:
            g = g - rt[r : r + CH, :].astype(f32)
        iout[r : r + CH, :] = g
    outs.append(io.start(iout, ig))
    for r in range(0, TXT, CH):
        wout[r : r + CH, :] = tn(t[:, r : r + CH], pre[...])
    outs.append(io.start(wout, wt))
    for copy in outs:
        copy.wait()


def first_call(i1, t0, t1a, t1b, t2a, t2b, ri0, rt0, zt0, lse_i, lse_t, hi, ht):
    n = ROWS
    return pl.pallas_call(
        first_kernel,
        out_shape=(wide(n), narrow(n), narrow(n), narrow(n), wide(n), wide(2 * n), wide(TXT)),
        in_specs=[ANY] * 9 + [VMEM] * 2 + [ANY] * 2,
        out_specs=(ANY,) * 7,
        scratch_shapes=[
            pltpu.VMEM((2 * n, EMB), bf16),
            pltpu.VMEM((2 * n, 128), f32),
            pltpu.VMEM((3 * n, TXT), bf16),
            pltpu.VMEM((3 * n, EMB), bf16),
            pltpu.VMEM((3 * n, EMB), f32),
            pltpu.VMEM((2 * n, 3 * n), bf16),
            pltpu.VMEM((3 * n, EMB), bf16),
            pltpu.VMEM((n, VIS), bf16),
            pltpu.VMEM((VIS, EMB), bf16),
            pltpu.VMEM((TXT, EMB), bf16),
            pltpu.VMEM((PAD, VIS), bf16),
            pltpu.VMEM((2, PAD, TXT), bf16),
            pltpu.VMEM((n, EMB), f32),
            pltpu.VMEM((n, EMB), f32),
            pltpu.VMEM((2, n, EMB), bf16),
            pltpu.VMEM((2 * n, EMB), f32),
            pltpu.VMEM((TXT, EMB), f32),
            pltpu.SemaphoreType.DMA((24,)),
        ],
        compiler_params=pltpu.CompilerParams(vmem_limit_bytes=48 * 1024 * 1024),
        cost_estimate=pl.CostEstimate(flops=12 * 10**9, bytes_accessed=20 * 10**6, transcendentals=2 * 10**6),
        name="first",
    )(i1, t0, t1a, t1b, t2a, t2b, ri0, rt0, zt0, lse_i, lse_t, hi, ht)


def second_kernel(core, i0, i1, t3a, t3b, p1, p2, ri0, ri1, zi0, zi1, ig, wt, lse_i, ht,
                  up, down, ipart, ibase, send, keep,
                  ri, ea, t, rt, zt, w, pre, prei, image, head_t, itail, ttail, zi, gi, wsum,
                  ubuf, dbuf, qout, bout, sout, kout, sems):
    io = Copies(sems)
    n = ROWS
    c_t = [io.start(t3a, t.at[pl.ds(0, MID)]), io.start(t3b.at[pl.ds(0, n - MID)], t.at[pl.ds(MID, n - MID)])]
    c_ht = io.start(ht, head_t)
    c_itail = io.start(i1.at[pl.ds(n, PAD)], itail)
    c_ttail = io.start(t3b.at[pl.ds(n - MID, PAD)], ttail)
    c_ri = [io.start(ri0, ri.at[pl.ds(0, n)]), io.start(ri1, ri.at[pl.ds(n, n)])]
    c_ig = io.start(ig, gi)
    c_zi = [io.start(zi0, zi.at[pl.ds(0, n)]), io.start(zi1, zi.at[pl.ds(n, n)])]
    c_image = [io.start(i0, image.at[pl.ds(0, n)]), io.start(i1.at[pl.ds(0, n)], image.at[pl.ds(n, n)])]
    c_wt = io.start(wt, wsum)
    c_p = [io.start(p2, ubuf.at[pl.ds(0, n)]), io.start(p1, dbuf.at[pl.ds(0, n)])]
    outs = []

    c_itail.wait()
    ea[0:n, :] = column_weights(lse_i[...])
    ea[n : 2 * n, :] = column_weights(image_tail(itail))
    for copy in c_t:
        copy.wait()
    c_ht.wait()
    for c in CHUNKS:
        raw = nn(t[c : c + CH, :], head_t[...])
        zt[c : c + CH, :] = raw
        rt[c : c + CH, :] = (raw * scale_of(raw)).astype(bf16)
    c_ttail.wait()
    for copy in c_ri:
        copy.wait()
    fill_weights(ri, rt[...], ea, text_tail(ttail), w, 0)
    for c in CHUNKS:
        g = tn(w[:, c : c + CH], ri[...])
        (ubuf, dbuf)[c // MID][n : n + MID, :] = g.astype(bf16)
        pre[c : c + CH, :] = pre_gradient(zt[c : c + CH, :], logit_scale * g)
    for copy in c_p:
        copy.wait()
    outs.append(io.start(ubuf, up))
    outs.append(io.start(dbuf, down))
    c_ig.wait()
    for copy in c_zi:
        copy.wait()
    for r in range(0, 2 * n, CH):
        g = gi[r : r + CH, :] + nn(w[r : r + CH, :], rt[...])
        if r < n:
            bout[r : r + CH, :] = g
        else:
            qout[r - n : r - n + CH, :] = g.astype(bf16)
        prei[r : r + CH, :] = pre_gradient(zi[r : r + CH, :], logit_scale * g)
    outs.append(io.start(bout, ibase))
    outs.append(io.start(qout, ipart))
    for copy in c_image:
        copy.wait()
    c_wt.wait()
    mine = core[0]
    for which, ref, out in ((1 - mine, sout, send), (mine, kout, keep)):
        for c in range(0, HV, CH):
            cols = pl.ds(pl.multiple_of(which * HV + c, 128), CH)
            ref[c : c + CH, :] = tn(image[:, cols], prei[...]).astype(ref.dtype)
        for c in range(0, HT, 128):
            cols = pl.ds(pl.multiple_of(which * HT + c, 128), 128)
            ref[HV + c : HV + c + 128, :] = (wsum[cols, :] + tn(t[:, cols], pre[...])).astype(ref.dtype)
        outs.append(io.start(ref, out))
    for copy in outs:
        copy.wait()


def second_call(core, i0, i1, t3a, t3b, p1, p2, ri0, ri1, zi0, zi1, ig, wt, lse_i, ht):
    n = ROWS
    return pl.pallas_call(
        second_kernel,
        out_shape=(narrow(n + MID), narrow(n + MID), narrow(n), wide(n), narrow(HALF), narrow(HALF)),
        in_specs=[SMEM] + [ANY] * 12 + [VMEM] + [ANY],
        out_specs=(ANY,) * 6,
        scratch_shapes=[
            pltpu.VMEM((2 * n, EMB), bf16),
            pltpu.VMEM((2 * n, 128), f32),
            pltpu.VMEM((n, TXT), bf16),
            pltpu.VMEM((n, EMB), bf16),
            pltpu.VMEM((n, EMB), f32),
            pltpu.VMEM((2 * n, n), bf16),
            pltpu.VMEM((n, EMB), bf16),
            pltpu.VMEM((2 * n, EMB), bf16),
            pltpu.VMEM((2 * n, VIS), bf16),
            pltpu.VMEM((TXT, EMB), bf16),
            pltpu.VMEM((PAD, VIS), bf16),
            pltpu.VMEM((PAD, TXT), bf16),
            pltpu.VMEM((2 * n, EMB), f32),
            pltpu.VMEM((2 * n, EMB), f32),
            pltpu.VMEM((TXT, EMB), f32),
            pltpu.VMEM((n + MID, EMB), bf16),
            pltpu.VMEM((n + MID, EMB), bf16),
            pltpu.VMEM((n, EMB), bf16),
            pltpu.VMEM((n, EMB), f32),
            pltpu.VMEM((HALF, EMB), bf16),
            pltpu.VMEM((HALF, EMB), bf16),
            pltpu.SemaphoreType.DMA((24,)),
        ],
        compiler_params=pltpu.CompilerParams(vmem_limit_bytes=48 * 1024 * 1024),
        cost_estimate=pl.CostEstimate(flops=8 * 10**9, bytes_accessed=20 * 10**6, transcendentals=10**6),
        name="second",
    )(core, i0, i1, t3a, t3b, p1, p2, ri0, ri1, zi0, zi1, ig, wt, lse_i, ht)


def back_kernel(whole, split, raw, head, base, *rest):
    out = rest[-1]
    for i, c in enumerate(CHUNKS):
        g = base[c : c + CH, :]
        for p in rest[:whole]:
            g = g + p[c : c + CH, :].astype(f32)
        if split:
            g = g + rest[whole + i][...].astype(f32)
        out[c : c + CH, :] = nt(pre_gradient(raw[c : c + CH, :], logit_scale * g), head[...])


def back_call(raw, head, base, parts, halves=()):
    width = head.shape[0]
    return pl.pallas_call(
        functools.partial(back_kernel, len(parts), len(halves) > 0),
        out_shape=wide(ROWS, width),
        in_specs=[VMEM] * (3 + len(parts) + len(halves)),
        out_specs=VMEM,
        compiler_params=pltpu.CompilerParams(vmem_limit_bytes=40 * 1024 * 1024),
        cost_estimate=pl.CostEstimate(flops=2 * ROWS * EMB * width, bytes_accessed=10 * 10**6, transcendentals=0),
        name="back",
    )(raw, head, base, *parts, *halves)


def final_kernel(first, core, half, *rest):
    image, text, buf, sems = rest[-4:]
    io = Copies(sems)
    which = core[0] if first else 1 - core[0]
    buf[...] = half[...].astype(f32)
    copies = [
        io.start(buf.at[pl.ds(0, HV)], image.at[pl.ds(pl.multiple_of(which * HV, 128), HV)]),
        io.start(buf.at[pl.ds(HV, HT)], text.at[pl.ds(pl.multiple_of(which * HT, 128), HT)]),
    ]
    for copy in copies:
        copy.wait()


def final_call(core, half, *written):
    return pl.pallas_call(
        functools.partial(final_kernel, len(written) == 0),
        out_shape=(wide(VIS), wide(TXT)),
        in_specs=[SMEM, VMEM] + [ANY] * len(written),
        out_specs=(ANY, ANY),
        scratch_shapes=[pltpu.VMEM((HALF, EMB), f32), pltpu.SemaphoreType.DMA((2,))],
        input_output_aliases={2: 0, 3: 1} if written else {},
        compiler_params=pltpu.CompilerParams(vmem_limit_bytes=32 * 1024 * 1024),
        cost_estimate=pl.CostEstimate(flops=10**6, bytes_accessed=4 * 10**6, transcendentals=0),
        name="final",
    )(core, half, *written)


def merge_kernel(a, b, out):
    for r in range(0, HALF, 128):
        out[r : r + 128, :] = (a[r : r + 128, :].astype(f32) + b[r : r + 128, :].astype(f32)).astype(bf16)


def merge_call(a, b):
    return pl.pallas_call(
        merge_kernel,
        out_shape=narrow(HALF),
        in_specs=[VMEM] * 2,
        out_specs=VMEM,
        compiler_params=pltpu.CompilerParams(vmem_limit_bytes=32 * 1024 * 1024),
        cost_estimate=pl.CostEstimate(flops=10**6, bytes_accessed=4 * 10**6, transcendentals=0),
        name="merge",
    )(a, b)


def total_kernel(own, plus, minus, across, out):
    total = (own[...].astype(f32) + across[...].astype(f32)) + (plus[...].astype(f32) + minus[...].astype(f32))
    total = total.astype(bf16)
    for k in range(16):
        out[k] = total


def total_call(*parts):
    return pl.pallas_call(
        total_kernel,
        out_shape=jax.ShapeDtypeStruct((16, HALF // 16, EMB), bf16),
        in_specs=[VMEM] * 4,
        out_specs=VMEM,
        compiler_params=pltpu.CompilerParams(vmem_limit_bytes=16 * 1024 * 1024),
        cost_estimate=pl.CostEstimate(flops=10**6, bytes_accessed=2 * 10**6, transcendentals=0),
        name="total",
    )(*parts)


def reduce_heads(send, keep):
    part = merge_call(keep, permute(send, "core", 2, 1)).reshape(16, HALF // 16, EMB)
    part = lax.all_to_all(part, PLANE, 0, 0, tiled=True)
    return jnp.sum(part.astype(f32), axis=0).astype(bf16)


def spread_heads(part, *beside):
    whole = total_call(part, *[permute(part, "y", 4, d) for d in (1, 3, 2)])
    whole, *beside = lax.optimization_barrier((whole, *beside))
    return lax.all_to_all(whole, PLANE, 0, 0, tiled=True).reshape(HALF, EMB), *beside


def shards(image_feats, text_feats, image_head, text_head, image_lse, text_lse):
    image_rows = image_feats[0]
    text_rows = text_feats[0]
    core = lax.axis_index("core").astype(jnp.int32).reshape(1)

    text_a, text_b, image_msg = pack_call(text_rows, image_rows, text_lse, image_lse)
    t1a = permute(text_a, "y", 4, 1)
    t2b = permute(text_b, "y", 4, 3)
    t1b = permute(text_b, "y", 4, 1)
    t2a = permute(text_a, "y", 4, 3)
    i1 = permute(image_msg, "xl", 2, 1)
    zi0, ri0, zt0, rt0 = own_call(image_rows, text_rows, image_head, text_head)
    t1a, t2b, zi0, ri0, zt0, rt0 = lax.optimization_barrier((t1a, t2b, zi0, ri0, zt0, rt0))
    t3a = permute(t1a, "y", 4, 1)
    t3b = permute(t2b, "y", 4, 3)

    tbase, p1, p2, ri1, zi1, ig, wt = first_call(
        i1, text_rows, t1a, t1b, t2a, t2b, ri0, rt0, zt0, image_lse, text_lse, image_head, text_head
    )
    up, down, ipart, ibase, send, keep = second_call(
        core, image_rows, i1, t3a, t3b, p1, p2, ri0, ri1, zi0, zi1, ig, wt, image_lse, text_head
    )
    part = reduce_heads(send, keep)
    up, down, ipart = permute(up, "y", 4, 1), permute(down, "y", 4, 3), permute(ipart, "xl", 2, 1)
    whole, up, down, ipart = spread_heads(part, up, down, ipart)
    top, bottom = permute(up[ROWS:], "y", 4, 1), permute(down[ROWS:], "y", 4, 3)
    text_back = back_call(zt0, text_head, tbase, [up, down], [top, bottom])
    image_back = back_call(zi0, image_head, ibase, [ipart])
    whole, text_back, image_back = lax.optimization_barrier((whole, text_back, image_back))
    other = permute(whole, "core", 2, 1)
    image_total, text_total = final_call(core, other, *final_call(core, whole))
    return (image_back[None], text_back[None], image_total, text_total)


def solution(mesh):
    finer = Mesh(mesh.devices.reshape(4, 2, 4, 2, 2), BLK + REP)
    return jax.shard_map(
        shards,
        mesh=finer,
        in_specs=(P(REP, BLK, None), P(REP, BLK, None), P(), P(), P(REP, BLK), P(REP, BLK)),
        out_specs=(P(REP, BLK, None), P(REP, BLK, None), P(), P()),
        check_vma=False,
    )
```

```python
import functools
import math

import jax
import jax.numpy as jnp
from jax import lax
from jax.experimental import pallas as pl
from jax.experimental.pallas import tpu as pltpu
from jax.sharding import Mesh
from jax.sharding import PartitionSpec as P

BLK = ("y", "xl")
REP = ("z", "xh", "core")
PLANE = ("xl", "z", "xh")

bf16 = jnp.bfloat16
f32 = jnp.float32

logit_scale = 50.0
epsilon = 1e-06
exp2_scale = logit_scale * math.log2(math.e)

ROWS = 512
PAD = 16
EMB = 768
VIS = 1024
TXT = 768
HV = VIS // 2
HT = TXT // 2
HALF = HV + HT


def permute(value, axis, size, shift):
    return lax.ppermute(value, axis, [(i, (i + shift) % size) for i in range(size)])


def nt(a, b):
    return lax.dot_general(a, b, (((1,), (1,)), ((), ())), preferred_element_type=f32)


def tn(a, b):
    return lax.dot_general(a, b, (((0,), (0,)), ((), ())), preferred_element_type=f32)


def nn(a, b):
    return jnp.dot(a, b, preferred_element_type=f32)


def scale_of(raw):
    return lax.rsqrt(jnp.sum(raw * raw, axis=1, keepdims=True) + epsilon)


def pre_gradient(raw, grad):
    factor = scale_of(raw)
    embed = raw * factor
    inner = jnp.sum(embed * grad, axis=1, keepdims=True)
    return (factor * (grad - embed * inner)).astype(bf16)


CH = 256
MID = ROWS // 2
CHUNKS = range(0, ROWS, CH)
ANY = pl.BlockSpec(memory_space=pl.ANY)
VMEM = pl.BlockSpec(memory_space=pltpu.VMEM)
SMEM = pl.BlockSpec(memory_space=pltpu.SMEM)
LIMIT = pltpu.CompilerParams(vmem_limit_bytes=48 * 1024 * 1024)
MOST = pltpu.CompilerParams(vmem_limit_bytes=60 * 1024 * 1024)


def wide(rows, columns=EMB):
    return jax.ShapeDtypeStruct((rows, columns), f32)


def narrow(rows, columns=EMB):
    return jax.ShapeDtypeStruct((rows, columns), bf16)


class Copies:
    def __init__(self, sems):
        self.sems = sems
        self.count = 0

    def start(self, src, dst):
        copy = pltpu.make_async_copy(src, dst, self.sems.at[self.count])
        self.count += 1
        copy.start()
        return copy


def pack_kernel(text, image, lse_t, lse_i, text_a, text_b, image_msg):
    n = ROWS
    text_a[...] = text[0:MID, :]
    text_b[0 : n - MID, :] = text[MID:n, :]
    row = lax.broadcasted_iota(jnp.int32, (PAD, n), 0)
    high = lse_t[...].astype(bf16).astype(f32)
    text_b[n - MID :, 0:n] = jnp.where(row == 0, high, lse_t[...] - high).astype(bf16)
    text_b[n - MID :, n:TXT] = jnp.zeros((PAD, TXT - n), bf16)
    image_msg[0:n, :] = image[...]
    high = lse_i[...].astype(bf16).astype(f32)
    image_msg[n:, 0:n] = jnp.broadcast_to(high, (PAD, n)).astype(bf16)
    image_msg[n:, n : 2 * n] = jnp.broadcast_to(lse_i[...] - high, (PAD, n)).astype(bf16)


def pack_call(text, image, lse_t, lse_i):
    return pl.pallas_call(
        pack_kernel,
        out_shape=(narrow(MID, TXT), narrow(ROWS - MID + PAD, TXT), narrow(ROWS + PAD, VIS)),
        in_specs=[VMEM] * 4,
        out_specs=(VMEM,) * 3,
        compiler_params=MOST,
        cost_estimate=pl.CostEstimate(flops=10**5, bytes_accessed=4 * 10**6, transcendentals=0),
        name="pack",
    )(text, image, lse_t, lse_i)


def own_kernel(image, text, hi, ht, zi, ri, zt, rt):
    for feats, head, raw_ref, round_ref in ((image, hi, zi, ri), (text, ht, zt, rt)):
        for c in CHUNKS:
            raw = nn(feats[c : c + CH, :], head[...])
            raw_ref[c : c + CH, :] = raw
            round_ref[c : c + CH, :] = (raw * scale_of(raw)).astype(bf16)


def own_call(image, text, hi, ht):
    return pl.pallas_call(
        own_kernel,
        out_shape=(wide(ROWS), narrow(ROWS), wide(ROWS), narrow(ROWS)),
        in_specs=[VMEM] * 4,
        out_specs=(VMEM,) * 4,
        compiler_params=LIMIT,
        cost_estimate=pl.CostEstimate(flops=14 * 10**8, bytes_accessed=10**7, transcendentals=0),
        name="own",
    )(image, text, hi, ht)


def column_weights(lse_row):
    row = 0.5 * jnp.exp(-lse_row)
    return jnp.broadcast_to(row, (128, ROWS)).T


def image_tail(tail):
    tail = tail[...].astype(f32)
    return tail[0:1, 0:ROWS] + tail[0:1, ROWS : 2 * ROWS]


def text_tail(tail):
    tail = tail[...].astype(f32)
    return tail[0:1, 0:ROWS] + tail[1:2, 0:ROWS]


def fill_weights(ri, rt_block, ea, lse_row, w, column):
    eb = 0.5 * jnp.exp(-lse_row)
    for r in range(0, 2 * ROWS, CH):
        s = nt(ri[r : r + CH, :], rt_block)
        both = jnp.concatenate([ea[r : r + CH, :]] * (ROWS // 128), axis=1) + eb
        w[r : r + CH, column : column + ROWS] = (jnp.exp2(s * exp2_scale) * both).astype(bf16)


def first_kernel(i1, t0, t1a, t1b, t2a, t2b, ri0, rt0, zt0, lse_i, lse_t, hi, ht,
                 tbase, p1, p2, ri1, zi1, ig, wt,
                 ri, ea, t, rt, zt, w, pre, image, head_i, head_t, itail, ttail, zout, bout, pout, iout, wout, sems):
    io = Copies(sems)
    n = ROWS
    c_image = io.start(i1.at[pl.ds(0, n)], image)
    c_hi = io.start(hi, head_i)
    c_itail = io.start(i1.at[pl.ds(n, PAD)], itail)
    c_rt0 = io.start(rt0, rt.at[pl.ds(0, n)])
    c_ri0 = io.start(ri0, ri.at[pl.ds(0, n)])
    c_zt0 = io.start(zt0, zt.at[pl.ds(0, n)])
    c_t = [[io.start(t0, t.at[pl.ds(0, n)])]]
    c_ht = io.start(ht, head_t)
    c_tail = []
    for b, top, low in ((1, t1a, t1b), (2, t2a, t2b)):
        c_t.append([
            io.start(top, t.at[pl.ds(b * n, MID)]),
            io.start(low.at[pl.ds(0, n - MID)], t.at[pl.ds(b * n + MID, n - MID)]),
        ])
        c_tail.append(io.start(low.at[pl.ds(n - MID, PAD)], ttail.at[b - 1]))
    outs = []

    c_image.wait()
    c_hi.wait()
    for c in CHUNKS:
        raw = nn(image[c : c + CH, :], head_i[...])
        zout[c : c + CH, :] = raw
        ri[n + c : n + c + CH, :] = (raw * scale_of(raw)).astype(bf16)
    for copy in [c_itail, c_rt0, c_ri0, c_zt0, c_ht, *c_tail, *c_t[0], *c_t[1], *c_t[2]]:
        copy.wait()
    ea[0:n, :] = column_weights(lse_i[...])
    ea[n : 2 * n, :] = column_weights(image_tail(itail))
    for b in range(3):
        at = b * n
        if b == 0:
            lse_row = lse_t[...]
        else:
            for c in CHUNKS:
                raw = nn(t[at + c : at + c + CH, :], head_t[...])
                zt[at + c : at + c + CH, :] = raw
                rt[at + c : at + c + CH, :] = (raw * scale_of(raw)).astype(bf16)
            lse_row = text_tail(ttail.at[b - 1])
        fill_weights(ri, rt[at : at + n, :], ea, lse_row, w, at)
        for c in CHUNKS:
            g = tn(w[:, at + c : at + c + CH], ri[...])
            if b == 0:
                g = g - ri[c : c + CH, :].astype(f32)
                bout[c : c + CH, :] = g
            else:
                pout[b - 1, c : c + CH, :] = g.astype(bf16)
            pre[at + c : at + c + CH, :] = pre_gradient(zt[at + c : at + c + CH, :], logit_scale * g)
    outs.append(io.start(zout, zi1))
    outs.append(io.start(ri.at[pl.ds(n, n)], ri1))
    outs.append(io.start(bout, tbase))
    outs.append(io.start(pout.at[0], p1))
    outs.append(io.start(pout.at[1], p2))
    for r in range(0, 2 * n, CH):
        g = nn(w[r : r + CH, :], rt[...])
        if r < n:
            g = g - rt[r : r + CH, :].astype(f32)
        iout[r : r + CH, :] = g
    outs.append(io.start(iout, ig))
    for r in range(0, TXT, CH):
        wout[r : r + CH, :] = tn(t[:, r : r + CH], pre[...])
        if r + CH == TXT - CH:
            outs.append(io.start(wout.at[pl.ds(0, TXT - CH)], wt.at[pl.ds(0, TXT - CH)]))
    outs.append(io.start(wout.at[pl.ds(TXT - CH, CH)], wt.at[pl.ds(TXT - CH, CH)]))
    for copy in outs:
        copy.wait()


def first_call(i1, t0, t1a, t1b, t2a, t2b, ri0, rt0, zt0, lse_i, lse_t, hi, ht):
    n = ROWS
    return pl.pallas_call(
        first_kernel,
        out_shape=(wide(n), narrow(n), narrow(n), narrow(n), wide(n), wide(2 * n), wide(TXT)),
        in_specs=[ANY] * 9 + [VMEM] * 2 + [ANY] * 2,
        out_specs=(ANY,) * 7,
        scratch_shapes=[
            pltpu.VMEM((2 * n, EMB), bf16),
            pltpu.VMEM((2 * n, 128), f32),
            pltpu.VMEM((3 * n, TXT), bf16),
            pltpu.VMEM((3 * n, EMB), bf16),
            pltpu.VMEM((3 * n, EMB), f32),
            pltpu.VMEM((2 * n, 3 * n), bf16),
            pltpu.VMEM((3 * n, EMB), bf16),
            pltpu.VMEM((n, VIS), bf16),
            pltpu.VMEM((VIS, EMB), bf16),
            pltpu.VMEM((TXT, EMB), bf16),
            pltpu.VMEM((PAD, VIS), bf16),
            pltpu.VMEM((2, PAD, TXT), bf16),
            pltpu.VMEM((n, EMB), f32),
            pltpu.VMEM((n, EMB), f32),
            pltpu.VMEM((2, n, EMB), bf16),
            pltpu.VMEM((2 * n, EMB), f32),
            pltpu.VMEM((TXT, EMB), f32),
            pltpu.SemaphoreType.DMA((24,)),
        ],
        compiler_params=pltpu.CompilerParams(vmem_limit_bytes=48 * 1024 * 1024),
        cost_estimate=pl.CostEstimate(flops=12 * 10**9, bytes_accessed=20 * 10**6, transcendentals=2 * 10**6),
        name="first",
    )(i1, t0, t1a, t1b, t2a, t2b, ri0, rt0, zt0, lse_i, lse_t, hi, ht)


def second_kernel(core, i0, i1, t3a, t3b, p1, p2, ri0, ri1, zi0, zi1, ig, wt, lse_i, ht,
                  up, down, ipart, ibase, send, keep,
                  ri, ea, t, rt, zt, w, pre, prei, image, head_t, itail, ttail, zi, gi, wsum,
                  ubuf, dbuf, qout, bout, sout, kout, sems):
    io = Copies(sems)
    n = ROWS
    c_t = [io.start(t3a, t.at[pl.ds(0, MID)]), io.start(t3b.at[pl.ds(0, n - MID)], t.at[pl.ds(MID, n - MID)])]
    c_ht = io.start(ht, head_t)
    c_itail = io.start(i1.at[pl.ds(n, PAD)], itail)
    c_ttail = io.start(t3b.at[pl.ds(n - MID, PAD)], ttail)
    c_ri = [io.start(ri0, ri.at[pl.ds(0, n)]), io.start(ri1, ri.at[pl.ds(n, n)])]
    c_ig = io.start(ig, gi)
    c_zi = [io.start(zi0, zi.at[pl.ds(0, n)]), io.start(zi1, zi.at[pl.ds(n, n)])]
    c_image = [io.start(i0, image.at[pl.ds(0, n)]), io.start(i1.at[pl.ds(0, n)], image.at[pl.ds(n, n)])]
    c_wt = io.start(wt, wsum)
    c_p = [io.start(p2, ubuf.at[pl.ds(0, n)]), io.start(p1, dbuf.at[pl.ds(0, n)])]
    outs = []

    c_itail.wait()
    ea[0:n, :] = column_weights(lse_i[...])
    ea[n : 2 * n, :] = column_weights(image_tail(itail))
    for copy in c_t:
        copy.wait()
    c_ht.wait()
    for c in CHUNKS:
        raw = nn(t[c : c + CH, :], head_t[...])
        zt[c : c + CH, :] = raw
        rt[c : c + CH, :] = (raw * scale_of(raw)).astype(bf16)
    c_ttail.wait()
    for copy in c_ri:
        copy.wait()
    fill_weights(ri, rt[...], ea, text_tail(ttail), w, 0)
    for c in CHUNKS:
        g = tn(w[:, c : c + CH], ri[...])
        (ubuf, dbuf)[c // MID][n : n + MID, :] = g.astype(bf16)
        pre[c : c + CH, :] = pre_gradient(zt[c : c + CH, :], logit_scale * g)
    for copy in c_p:
        copy.wait()
    outs.append(io.start(ubuf, up))
    outs.append(io.start(dbuf, down))
    c_ig.wait()
    for copy in c_zi:
        copy.wait()
    for r in range(0, 2 * n, CH):
        g = gi[r : r + CH, :] + nn(w[r : r + CH, :], rt[...])
        if r < n:
            bout[r : r + CH, :] = g
        else:
            qout[r - n : r - n + CH, :] = g.astype(bf16)
        prei[r : r + CH, :] = pre_gradient(zi[r : r + CH, :], logit_scale * g)
    outs.append(io.start(bout, ibase))
    outs.append(io.start(qout, ipart))
    for copy in c_image:
        copy.wait()
    c_wt.wait()
    mine = core[0]
    for which, ref, out in ((1 - mine, sout, send), (mine, kout, keep)):
        for c in range(0, HV, CH):
            cols = pl.ds(pl.multiple_of(which * HV + c, 128), CH)
            ref[c : c + CH, :] = tn(image[:, cols], prei[...]).astype(ref.dtype)
        for c in range(0, HT, 128):
            cols = pl.ds(pl.multiple_of(which * HT + c, 128), 128)
            ref[HV + c : HV + c + 128, :] = (wsum[cols, :] + tn(t[:, cols], pre[...])).astype(ref.dtype)
        outs.append(io.start(ref, out))
    for copy in outs:
        copy.wait()


def second_call(core, i0, i1, t3a, t3b, p1, p2, ri0, ri1, zi0, zi1, ig, wt, lse_i, ht):
    n = ROWS
    return pl.pallas_call(
        second_kernel,
        out_shape=(narrow(n + MID), narrow(n + MID), narrow(n), wide(n), narrow(HALF), narrow(HALF)),
        in_specs=[SMEM] + [ANY] * 12 + [VMEM] + [ANY],
        out_specs=(ANY,) * 6,
        scratch_shapes=[
            pltpu.VMEM((2 * n, EMB), bf16),
            pltpu.VMEM((2 * n, 128), f32),
            pltpu.VMEM((n, TXT), bf16),
            pltpu.VMEM((n, EMB), bf16),
            pltpu.VMEM((n, EMB), f32),
            pltpu.VMEM((2 * n, n), bf16),
            pltpu.VMEM((n, EMB), bf16),
            pltpu.VMEM((2 * n, EMB), bf16),
            pltpu.VMEM((2 * n, VIS), bf16),
            pltpu.VMEM((TXT, EMB), bf16),
            pltpu.VMEM((PAD, VIS), bf16),
            pltpu.VMEM((PAD, TXT), bf16),
            pltpu.VMEM((2 * n, EMB), f32),
            pltpu.VMEM((2 * n, EMB), f32),
            pltpu.VMEM((TXT, EMB), f32),
            pltpu.VMEM((n + MID, EMB), bf16),
            pltpu.VMEM((n + MID, EMB), bf16),
            pltpu.VMEM((n, EMB), bf16),
            pltpu.VMEM((n, EMB), f32),
            pltpu.VMEM((HALF, EMB), bf16),
            pltpu.VMEM((HALF, EMB), bf16),
            pltpu.SemaphoreType.DMA((24,)),
        ],
        compiler_params=pltpu.CompilerParams(vmem_limit_bytes=48 * 1024 * 1024),
        cost_estimate=pl.CostEstimate(flops=8 * 10**9, bytes_accessed=20 * 10**6, transcendentals=10**6),
        name="second",
    )(core, i0, i1, t3a, t3b, p1, p2, ri0, ri1, zi0, zi1, ig, wt, lse_i, ht)


def back_kernel(whole, split, raw, head, base, *rest):
    out = rest[-1]
    for i, c in enumerate(CHUNKS):
        g = base[c : c + CH, :]
        for p in rest[:whole]:
            g = g + p[c : c + CH, :].astype(f32)
        if split:
            g = g + rest[whole + i][...].astype(f32)
        out[c : c + CH, :] = nt(pre_gradient(raw[c : c + CH, :], logit_scale * g), head[...])


def back_call(raw, head, base, parts, halves=()):
    width = head.shape[0]
    return pl.pallas_call(
        functools.partial(back_kernel, len(parts), len(halves) > 0),
        out_shape=wide(ROWS, width),
        in_specs=[VMEM] * (3 + len(parts) + len(halves)),
        out_specs=VMEM,
        compiler_params=pltpu.CompilerParams(vmem_limit_bytes=40 * 1024 * 1024),
        cost_estimate=pl.CostEstimate(flops=2 * ROWS * EMB * width, bytes_accessed=10 * 10**6, transcendentals=0),
        name="back",
    )(raw, head, base, *parts, *halves)


def final_kernel(first, core, half, *rest):
    image, text, buf, sems = rest[-4:]
    io = Copies(sems)
    which = core[0] if first else 1 - core[0]
    buf[...] = half[...].astype(f32)
    copies = [
        io.start(buf.at[pl.ds(0, HV)], image.at[pl.ds(pl.multiple_of(which * HV, 128), HV)]),
        io.start(buf.at[pl.ds(HV, HT)], text.at[pl.ds(pl.multiple_of(which * HT, 128), HT)]),
    ]
    for copy in copies:
        copy.wait()


def final_call(core, half, *written):
    return pl.pallas_call(
        functools.partial(final_kernel, len(written) == 0),
        out_shape=(wide(VIS), wide(TXT)),
        in_specs=[SMEM, VMEM] + [ANY] * len(written),
        out_specs=(ANY, ANY),
        scratch_shapes=[pltpu.VMEM((HALF, EMB), f32), pltpu.SemaphoreType.DMA((2,))],
        input_output_aliases={2: 0, 3: 1} if written else {},
        compiler_params=pltpu.CompilerParams(vmem_limit_bytes=32 * 1024 * 1024),
        cost_estimate=pl.CostEstimate(flops=10**6, bytes_accessed=4 * 10**6, transcendentals=0),
        name="final",
    )(core, half, *written)


def merge_kernel(a, b, out):
    for r in range(0, HALF, 128):
        out[r : r + 128, :] = (a[r : r + 128, :].astype(f32) + b[r : r + 128, :].astype(f32)).astype(bf16)


def merge_call(a, b):
    return pl.pallas_call(
        merge_kernel,
        out_shape=narrow(HALF),
        in_specs=[VMEM] * 2,
        out_specs=VMEM,
        compiler_params=pltpu.CompilerParams(vmem_limit_bytes=32 * 1024 * 1024),
        cost_estimate=pl.CostEstimate(flops=10**6, bytes_accessed=4 * 10**6, transcendentals=0),
        name="merge",
    )(a, b)


def total_kernel(own, plus, minus, across, out):
    total = (own[...].astype(f32) + across[...].astype(f32)) + (plus[...].astype(f32) + minus[...].astype(f32))
    total = total.astype(bf16)
    for k in range(16):
        out[k] = total


def total_call(*parts):
    return pl.pallas_call(
        total_kernel,
        out_shape=jax.ShapeDtypeStruct((16, HALF // 16, EMB), bf16),
        in_specs=[VMEM] * 4,
        out_specs=VMEM,
        compiler_params=pltpu.CompilerParams(vmem_limit_bytes=16 * 1024 * 1024),
        cost_estimate=pl.CostEstimate(flops=10**6, bytes_accessed=2 * 10**6, transcendentals=0),
        name="total",
    )(*parts)


def reduce_heads(send, keep):
    part = merge_call(keep, permute(send, "core", 2, 1)).reshape(16, HALF // 16, EMB)
    part = lax.all_to_all(part, PLANE, 0, 0, tiled=True)
    return jnp.sum(part.astype(f32), axis=0).astype(bf16)


def spread_heads(part, *beside):
    whole = total_call(part, *[permute(part, "y", 4, d) for d in (1, 3, 2)])
    whole, *beside = lax.optimization_barrier((whole, *beside))
    return lax.all_to_all(whole, PLANE, 0, 0, tiled=True).reshape(HALF, EMB), *beside


def shards(image_feats, text_feats, image_head, text_head, image_lse, text_lse):
    image_rows = image_feats[0]
    text_rows = text_feats[0]
    core = lax.axis_index("core").astype(jnp.int32).reshape(1)

    text_a, text_b, image_msg = pack_call(text_rows, image_rows, text_lse, image_lse)
    t1a = permute(text_a, "y", 4, 1)
    t2b = permute(text_b, "y", 4, 3)
    t1b = permute(text_b, "y", 4, 1)
    t2a = permute(text_a, "y", 4, 3)
    i1 = permute(image_msg, "xl", 2, 1)
    zi0, ri0, zt0, rt0 = own_call(image_rows, text_rows, image_head, text_head)
    t1a, t2b, zi0, ri0, zt0, rt0 = lax.optimization_barrier((t1a, t2b, zi0, ri0, zt0, rt0))
    t3a = permute(t1a, "y", 4, 1)
    t3b = permute(t2b, "y", 4, 3)

    tbase, p1, p2, ri1, zi1, ig, wt = first_call(
        i1, text_rows, t1a, t1b, t2a, t2b, ri0, rt0, zt0, image_lse, text_lse, image_head, text_head
    )
    up, down, ipart, ibase, send, keep = second_call(
        core, image_rows, i1, t3a, t3b, p1, p2, ri0, ri1, zi0, zi1, ig, wt, image_lse, text_head
    )
    part = reduce_heads(send, keep)
    up, down, ipart = permute(up, "y", 4, 1), permute(down, "y", 4, 3), permute(ipart, "xl", 2, 1)
    whole, up, down, ipart = spread_heads(part, up, down, ipart)
    top, bottom = permute(up[ROWS:], "y", 4, 1), permute(down[ROWS:], "y", 4, 3)
    text_back = back_call(zt0, text_head, tbase, [up, down], [top, bottom])
    image_back = back_call(zi0, image_head, ibase, [ipart])
    whole, text_back, image_back = lax.optimization_barrier((whole, text_back, image_back))
    other = permute(whole, "core", 2, 1)
    image_total, text_total = final_call(core, other, *final_call(core, whole))
    return (image_back[None], text_back[None], image_total, text_total)


def solution(mesh):
    finer = Mesh(mesh.devices.reshape(4, 2, 4, 2, 2), BLK + REP)
    return jax.shard_map(
        shards,
        mesh=finer,
        in_specs=(P(REP, BLK, None), P(REP, BLK, None), P(), P(), P(REP, BLK), P(REP, BLK)),
        out_specs=(P(REP, BLK, None), P(REP, BLK, None), P(), P()),
        check_vma=False,
    )
```

```python
import functools
import math

import jax
import jax.numpy as jnp
from jax import lax
from jax.experimental import pallas as pl
from jax.experimental.pallas import tpu as pltpu
from jax.sharding import Mesh
from jax.sharding import PartitionSpec as P

BLK = ("y", "xl")
REP = ("z", "xh", "core")
PLANE = ("xl", "z", "xh")

bf16 = jnp.bfloat16
f32 = jnp.float32

logit_scale = 50.0
epsilon = 1e-06
exp2_scale = logit_scale * math.log2(math.e)

ROWS = 512
PAD = 16
EMB = 768
VIS = 1024
TXT = 768
HV = VIS // 2
HT = TXT // 2
HALF = HV + HT


def permute(value, axis, size, shift):
    return lax.ppermute(value, axis, [(i, (i + shift) % size) for i in range(size)])


def nt(a, b):
    return lax.dot_general(a, b, (((1,), (1,)), ((), ())), preferred_element_type=f32)


def tn(a, b):
    return lax.dot_general(a, b, (((0,), (0,)), ((), ())), preferred_element_type=f32)


def nn(a, b):
    return jnp.dot(a, b, preferred_element_type=f32)


def scale_of(raw):
    return lax.rsqrt(jnp.sum(raw * raw, axis=1, keepdims=True) + epsilon)


def pre_gradient(raw, grad):
    factor = scale_of(raw)
    embed = raw * factor
    inner = jnp.sum(embed * grad, axis=1, keepdims=True)
    return (factor * (grad - embed * inner)).astype(bf16)


CH = 256
MID = ROWS // 2
CHUNKS = range(0, ROWS, CH)
ANY = pl.BlockSpec(memory_space=pl.ANY)
VMEM = pl.BlockSpec(memory_space=pltpu.VMEM)
SMEM = pl.BlockSpec(memory_space=pltpu.SMEM)
LIMIT = pltpu.CompilerParams(vmem_limit_bytes=48 * 1024 * 1024)
MOST = pltpu.CompilerParams(vmem_limit_bytes=60 * 1024 * 1024)


def wide(rows, columns=EMB):
    return jax.ShapeDtypeStruct((rows, columns), f32)


def narrow(rows, columns=EMB):
    return jax.ShapeDtypeStruct((rows, columns), bf16)


class Copies:
    def __init__(self, sems):
        self.sems = sems
        self.count = 0

    def start(self, src, dst):
        copy = pltpu.make_async_copy(src, dst, self.sems.at[self.count])
        self.count += 1
        copy.start()
        return copy


def pack_kernel(text, image, lse_t, lse_i, text_a, text_b, image_msg):
    n = ROWS
    text_a[...] = text[0:MID, :]
    text_b[0 : n - MID, :] = text[MID:n, :]
    row = lax.broadcasted_iota(jnp.int32, (PAD, n), 0)
    high = lse_t[...].astype(bf16).astype(f32)
    text_b[n - MID :, 0:n] = jnp.where(row == 0, high, lse_t[...] - high).astype(bf16)
    text_b[n - MID :, n:TXT] = jnp.zeros((PAD, TXT - n), bf16)
    image_msg[0:n, :] = image[...]
    high = lse_i[...].astype(bf16).astype(f32)
    image_msg[n:, 0:n] = jnp.broadcast_to(high, (PAD, n)).astype(bf16)
    image_msg[n:, n : 2 * n] = jnp.broadcast_to(lse_i[...] - high, (PAD, n)).astype(bf16)


def pack_call(text, image, lse_t, lse_i):
    return pl.pallas_call(
        pack_kernel,
        out_shape=(narrow(MID, TXT), narrow(ROWS - MID + PAD, TXT), narrow(ROWS + PAD, VIS)),
        in_specs=[VMEM] * 4,
        out_specs=(VMEM,) * 3,
        compiler_params=MOST,
        cost_estimate=pl.CostEstimate(flops=10**5, bytes_accessed=4 * 10**6, transcendentals=0),
        name="pack",
    )(text, image, lse_t, lse_i)


def own_kernel(image, text, hi, ht, zi, ri, zt, rt):
    for feats, head, raw_ref, round_ref in ((image, hi, zi, ri), (text, ht, zt, rt)):
        for c in CHUNKS:
            raw = nn(feats[c : c + CH, :], head[...])
            raw_ref[c : c + CH, :] = raw
            round_ref[c : c + CH, :] = (raw * scale_of(raw)).astype(bf16)


def own_call(image, text, hi, ht):
    return pl.pallas_call(
        own_kernel,
        out_shape=(wide(ROWS), narrow(ROWS), wide(ROWS), narrow(ROWS)),
        in_specs=[VMEM] * 4,
        out_specs=(VMEM,) * 4,
        compiler_params=LIMIT,
        cost_estimate=pl.CostEstimate(flops=14 * 10**8, bytes_accessed=10**7, transcendentals=0),
        name="own",
    )(image, text, hi, ht)


def column_weights(lse_row):
    row = 0.5 * jnp.exp(-lse_row)
    return jnp.broadcast_to(row, (128, ROWS)).T


def image_tail(tail):
    tail = tail[...].astype(f32)
    return tail[0:1, 0:ROWS] + tail[0:1, ROWS : 2 * ROWS]


def text_tail(tail):
    tail = tail[...].astype(f32)
    return tail[0:1, 0:ROWS] + tail[1:2, 0:ROWS]


def fill_weights(ri, rt_block, ea, lse_row, w, column):
    eb = 0.5 * jnp.exp(-lse_row)
    for r in range(0, 2 * ROWS, CH):
        s = nt(ri[r : r + CH, :], rt_block)
        both = jnp.concatenate([ea[r : r + CH, :]] * (ROWS // 128), axis=1) + eb
        w[r : r + CH, column : column + ROWS] = (jnp.exp2(s * exp2_scale) * both).astype(bf16)


def first_kernel(i1, t0, t1a, t1b, t2a, t2b, ri0, rt0, zt0, lse_i, lse_t, hi, ht,
                 tbase, p1, p2, ri1, zi1, ig, wt,
                 ri, ea, t, rt, zt, w, pre, image, head_i, head_t, itail, ttail, zout, bout, pout, iout, wout, sems):
    io = Copies(sems)
    n = ROWS
    c_image = io.start(i1.at[pl.ds(0, n)], image)
    c_hi = io.start(hi, head_i)
    c_itail = io.start(i1.at[pl.ds(n, PAD)], itail)
    c_rt0 = io.start(rt0, rt.at[pl.ds(0, n)])
    c_ri0 = io.start(ri0, ri.at[pl.ds(0, n)])
    c_zt0 = io.start(zt0, zt.at[pl.ds(0, n)])
    c_t = [[io.start(t0, t.at[pl.ds(0, n)])]]
    c_ht = io.start(ht, head_t)
    c_tail = []
    for b, top, low in ((1, t1a, t1b), (2, t2a, t2b)):
        c_t.append([
            io.start(top, t.at[pl.ds(b * n, MID)]),
            io.start(low.at[pl.ds(0, n - MID)], t.at[pl.ds(b * n + MID, n - MID)]),
        ])
        c_tail.append(io.start(low.at[pl.ds(n - MID, PAD)], ttail.at[b - 1]))
    outs = []

    c_image.wait()
    c_hi.wait()
    for c in CHUNKS:
        raw = nn(image[c : c + CH, :], head_i[...])
        zout[c : c + CH, :] = raw
        ri[n + c : n + c + CH, :] = (raw * scale_of(raw)).astype(bf16)
    for copy in [c_itail, c_rt0, c_ri0, c_zt0, c_ht, *c_tail, *c_t[0], *c_t[1], *c_t[2]]:
        copy.wait()
    ea[0:n, :] = column_weights(lse_i[...])
    ea[n : 2 * n, :] = column_weights(image_tail(itail))
    for b in range(3):
        at = b * n
        if b == 0:
            lse_row = lse_t[...]
        else:
            for c in CHUNKS:
                raw = nn(t[at + c : at + c + CH, :], head_t[...])
                zt[at + c : at + c + CH, :] = raw
                rt[at + c : at + c + CH, :] = (raw * scale_of(raw)).astype(bf16)
            lse_row = text_tail(ttail.at[b - 1])
        fill_weights(ri, rt[at : at + n, :], ea, lse_row, w, at)
        for c in CHUNKS:
            g = tn(w[:, at + c : at + c + CH], ri[...])
            if b == 0:
                g = g - ri[c : c + CH, :].astype(f32)
                bout[c : c + CH, :] = g
            else:
                pout[b - 1, c : c + CH, :] = g.astype(bf16)
            pre[at + c : at + c + CH, :] = pre_gradient(zt[at + c : at + c + CH, :], logit_scale * g)
    outs.append(io.start(zout, zi1))
    outs.append(io.start(ri.at[pl.ds(n, n)], ri1))
    outs.append(io.start(bout, tbase))
    outs.append(io.start(pout.at[0], p1))
    outs.append(io.start(pout.at[1], p2))
    for r in range(0, 2 * n, CH):
        g = nn(w[r : r + CH, :], rt[...])
        if r < n:
            g = g - rt[r : r + CH, :].astype(f32)
        iout[r : r + CH, :] = g
    outs.append(io.start(iout, ig))
    for r in range(0, TXT, CH):
        wout[r : r + CH, :] = tn(t[:, r : r + CH], pre[...])
        if r + CH == TXT - CH:
            outs.append(io.start(wout.at[pl.ds(0, TXT - CH)], wt.at[pl.ds(0, TXT - CH)]))
    outs.append(io.start(wout.at[pl.ds(TXT - CH, CH)], wt.at[pl.ds(TXT - CH, CH)]))
    for copy in outs:
        copy.wait()


def first_call(i1, t0, t1a, t1b, t2a, t2b, ri0, rt0, zt0, lse_i, lse_t, hi, ht):
    n = ROWS
    return pl.pallas_call(
        first_kernel,
        out_shape=(wide(n), narrow(n), narrow(n), narrow(n), wide(n), wide(2 * n), wide(TXT)),
        in_specs=[ANY] * 9 + [VMEM] * 2 + [ANY] * 2,
        out_specs=(ANY,) * 7,
        scratch_shapes=[
            pltpu.VMEM((2 * n, EMB), bf16),
            pltpu.VMEM((2 * n, 128), f32),
            pltpu.VMEM((3 * n, TXT), bf16),
            pltpu.VMEM((3 * n, EMB), bf16),
            pltpu.VMEM((3 * n, EMB), f32),
            pltpu.VMEM((2 * n, 3 * n), bf16),
            pltpu.VMEM((3 * n, EMB), bf16),
            pltpu.VMEM((n, VIS), bf16),
            pltpu.VMEM((VIS, EMB), bf16),
            pltpu.VMEM((TXT, EMB), bf16),
            pltpu.VMEM((PAD, VIS), bf16),
            pltpu.VMEM((2, PAD, TXT), bf16),
            pltpu.VMEM((n, EMB), f32),
            pltpu.VMEM((n, EMB), f32),
            pltpu.VMEM((2, n, EMB), bf16),
            pltpu.VMEM((2 * n, EMB), f32),
            pltpu.VMEM((TXT, EMB), f32),
            pltpu.SemaphoreType.DMA((24,)),
        ],
        compiler_params=pltpu.CompilerParams(vmem_limit_bytes=48 * 1024 * 1024),
        cost_estimate=pl.CostEstimate(flops=12 * 10**9, bytes_accessed=20 * 10**6, transcendentals=2 * 10**6),
        name="first",
    )(i1, t0, t1a, t1b, t2a, t2b, ri0, rt0, zt0, lse_i, lse_t, hi, ht)


def second_kernel(core, i0, i1, t3a, t3b, p1, p2, ri0, ri1, zi0, zi1, ig, wt, lse_i, ht,
                  up, down, ipart, ibase, send, keep,
                  ri, ea, t, rt, zt, w, pre, prei, image, head_t, itail, ttail, zi, gi, wsum,
                  ubuf, dbuf, qout, bout, sout, kout, sems):
    io = Copies(sems)
    n = ROWS
    c_t = [io.start(t3a, t.at[pl.ds(0, MID)]), io.start(t3b.at[pl.ds(0, n - MID)], t.at[pl.ds(MID, n - MID)])]
    c_ht = io.start(ht, head_t)
    c_itail = io.start(i1.at[pl.ds(n, PAD)], itail)
    c_ttail = io.start(t3b.at[pl.ds(n - MID, PAD)], ttail)
    c_ri = [io.start(ri0, ri.at[pl.ds(0, n)]), io.start(ri1, ri.at[pl.ds(n, n)])]
    c_ig = io.start(ig, gi)
    c_zi = [io.start(zi0, zi.at[pl.ds(0, n)]), io.start(zi1, zi.at[pl.ds(n, n)])]
    c_image = [io.start(i0, image.at[pl.ds(0, n)]), io.start(i1.at[pl.ds(0, n)], image.at[pl.ds(n, n)])]
    c_wt = io.start(wt, wsum)
    c_p = [io.start(p2, ubuf.at[pl.ds(0, n)]), io.start(p1, dbuf.at[pl.ds(0, n)])]
    outs = []

    c_itail.wait()
    ea[0:n, :] = column_weights(lse_i[...])
    ea[n : 2 * n, :] = column_weights(image_tail(itail))
    for copy in c_t:
        copy.wait()
    c_ht.wait()
    for c in CHUNKS:
        raw = nn(t[c : c + CH, :], head_t[...])
        zt[c : c + CH, :] = raw
        rt[c : c + CH, :] = (raw * scale_of(raw)).astype(bf16)
    c_ttail.wait()
    for copy in c_ri:
        copy.wait()
    fill_weights(ri, rt[...], ea, text_tail(ttail), w, 0)
    for c in CHUNKS:
        g = tn(w[:, c : c + CH], ri[...])
        (ubuf, dbuf)[c // MID][n : n + MID, :] = g.astype(bf16)
        pre[c : c + CH, :] = pre_gradient(zt[c : c + CH, :], logit_scale * g)
    for copy in c_p:
        copy.wait()
    outs.append(io.start(ubuf, up))
    outs.append(io.start(dbuf, down))
    c_ig.wait()
    for copy in c_zi:
        copy.wait()
    for r in range(0, 2 * n, CH):
        g = gi[r : r + CH, :] + nn(w[r : r + CH, :], rt[...])
        if r < n:
            bout[r : r + CH, :] = g
        else:
            qout[r - n : r - n + CH, :] = g.astype(bf16)
        prei[r : r + CH, :] = pre_gradient(zi[r : r + CH, :], logit_scale * g)
    outs.append(io.start(bout, ibase))
    outs.append(io.start(qout, ipart))
    for copy in c_image:
        copy.wait()
    c_wt.wait()
    mine = core[0]
    for which, ref, out in ((1 - mine, sout, send), (mine, kout, keep)):
        for c in range(0, HV, CH):
            cols = pl.ds(pl.multiple_of(which * HV + c, 128), CH)
            ref[c : c + CH, :] = tn(image[:, cols], prei[...]).astype(ref.dtype)
        for c in range(0, HT, 128):
            cols = pl.ds(pl.multiple_of(which * HT + c, 128), 128)
            ref[HV + c : HV + c + 128, :] = (wsum[cols, :] + tn(t[:, cols], pre[...])).astype(ref.dtype)
        outs.append(io.start(ref, out))
    for copy in outs:
        copy.wait()


def second_call(core, i0, i1, t3a, t3b, p1, p2, ri0, ri1, zi0, zi1, ig, wt, lse_i, ht):
    n = ROWS
    return pl.pallas_call(
        second_kernel,
        out_shape=(narrow(n + MID), narrow(n + MID), narrow(n), wide(n), narrow(HALF), narrow(HALF)),
        in_specs=[SMEM] + [ANY] * 12 + [VMEM] + [ANY],
        out_specs=(ANY,) * 6,
        scratch_shapes=[
            pltpu.VMEM((2 * n, EMB), bf16),
            pltpu.VMEM((2 * n, 128), f32),
            pltpu.VMEM((n, TXT), bf16),
            pltpu.VMEM((n, EMB), bf16),
            pltpu.VMEM((n, EMB), f32),
            pltpu.VMEM((2 * n, n), bf16),
            pltpu.VMEM((n, EMB), bf16),
            pltpu.VMEM((2 * n, EMB), bf16),
            pltpu.VMEM((2 * n, VIS), bf16),
            pltpu.VMEM((TXT, EMB), bf16),
            pltpu.VMEM((PAD, VIS), bf16),
            pltpu.VMEM((PAD, TXT), bf16),
            pltpu.VMEM((2 * n, EMB), f32),
            pltpu.VMEM((2 * n, EMB), f32),
            pltpu.VMEM((TXT, EMB), f32),
            pltpu.VMEM((n + MID, EMB), bf16),
            pltpu.VMEM((n + MID, EMB), bf16),
            pltpu.VMEM((n, EMB), bf16),
            pltpu.VMEM((n, EMB), f32),
            pltpu.VMEM((HALF, EMB), bf16),
            pltpu.VMEM((HALF, EMB), bf16),
            pltpu.SemaphoreType.DMA((24,)),
        ],
        compiler_params=pltpu.CompilerParams(vmem_limit_bytes=48 * 1024 * 1024),
        cost_estimate=pl.CostEstimate(flops=8 * 10**9, bytes_accessed=20 * 10**6, transcendentals=10**6),
        name="second",
    )(core, i0, i1, t3a, t3b, p1, p2, ri0, ri1, zi0, zi1, ig, wt, lse_i, ht)


def back_kernel(whole, split, raw, head, base, *rest):
    out = rest[-1]
    for i, c in enumerate(CHUNKS):
        g = base[c : c + CH, :]
        for p in rest[:whole]:
            g = g + p[c : c + CH, :].astype(f32)
        if split:
            g = g + rest[whole + i][...].astype(f32)
        out[c : c + CH, :] = nt(pre_gradient(raw[c : c + CH, :], logit_scale * g), head[...])


def back_call(raw, head, base, parts, halves=()):
    width = head.shape[0]
    return pl.pallas_call(
        functools.partial(back_kernel, len(parts), len(halves) > 0),
        out_shape=wide(ROWS, width),
        in_specs=[VMEM] * (3 + len(parts) + len(halves)),
        out_specs=VMEM,
        compiler_params=pltpu.CompilerParams(vmem_limit_bytes=40 * 1024 * 1024),
        cost_estimate=pl.CostEstimate(flops=2 * ROWS * EMB * width, bytes_accessed=10 * 10**6, transcendentals=0),
        name="back",
    )(raw, head, base, *parts, *halves)


def final_kernel(first, core, half, *rest):
    image, text, buf, sems = rest[-4:]
    io = Copies(sems)
    which = core[0] if first else 1 - core[0]
    buf[...] = half[...].astype(f32)
    copies = [
        io.start(buf.at[pl.ds(0, HV)], image.at[pl.ds(pl.multiple_of(which * HV, 128), HV)]),
        io.start(buf.at[pl.ds(HV, HT)], text.at[pl.ds(pl.multiple_of(which * HT, 128), HT)]),
    ]
    for copy in copies:
        copy.wait()


def final_call(core, half, *written):
    return pl.pallas_call(
        functools.partial(final_kernel, len(written) == 0),
        out_shape=(wide(VIS), wide(TXT)),
        in_specs=[SMEM, VMEM] + [ANY] * len(written),
        out_specs=(ANY, ANY),
        scratch_shapes=[pltpu.VMEM((HALF, EMB), f32), pltpu.SemaphoreType.DMA((2,))],
        input_output_aliases={2: 0, 3: 1} if written else {},
        compiler_params=pltpu.CompilerParams(vmem_limit_bytes=32 * 1024 * 1024),
        cost_estimate=pl.CostEstimate(flops=10**6, bytes_accessed=4 * 10**6, transcendentals=0),
        name="final",
    )(core, half, *written)


def merge_kernel(a, b, out):
    for r in range(0, HALF, 128):
        out[r : r + 128, :] = (a[r : r + 128, :].astype(f32) + b[r : r + 128, :].astype(f32)).astype(bf16)


def merge_call(a, b):
    return pl.pallas_call(
        merge_kernel,
        out_shape=narrow(HALF),
        in_specs=[VMEM] * 2,
        out_specs=VMEM,
        compiler_params=pltpu.CompilerParams(vmem_limit_bytes=32 * 1024 * 1024),
        cost_estimate=pl.CostEstimate(flops=10**6, bytes_accessed=4 * 10**6, transcendentals=0),
        name="merge",
    )(a, b)


def total_kernel(own, other, out):
    total = (own[...].astype(f32) + other[...].astype(f32)).astype(bf16)
    for k in range(16):
        out[k] = total


def total_call(*parts):
    return pl.pallas_call(
        total_kernel,
        out_shape=jax.ShapeDtypeStruct((16, HALF // 16, EMB), bf16),
        in_specs=[VMEM] * 2,
        out_specs=VMEM,
        compiler_params=pltpu.CompilerParams(vmem_limit_bytes=16 * 1024 * 1024),
        cost_estimate=pl.CostEstimate(flops=10**6, bytes_accessed=2 * 10**6, transcendentals=0),
        name="total",
    )(*parts)


def reduce_heads(send, keep):
    part = merge_call(keep, permute(send, "core", 2, 1)).reshape(16, HALF // 16, EMB)
    part = lax.all_to_all(part, PLANE, 0, 0, tiled=True)
    return jnp.sum(part.astype(f32), axis=0).astype(bf16)


def spread_heads(part, *beside):
    near = lax.ppermute(part, "y", [(0, 1), (1, 0), (2, 3), (3, 2)])
    part = (part.astype(f32) + near.astype(f32)).astype(bf16)
    whole = total_call(part, lax.ppermute(part, "y", [(0, 3), (3, 0), (1, 2), (2, 1)]))
    whole, *beside = lax.optimization_barrier((whole, *beside))
    return lax.all_to_all(whole, PLANE, 0, 0, tiled=True).reshape(HALF, EMB), *beside


def shards(image_feats, text_feats, image_head, text_head, image_lse, text_lse):
    image_rows = image_feats[0]
    text_rows = text_feats[0]
    core = lax.axis_index("core").astype(jnp.int32).reshape(1)

    text_a, text_b, image_msg = pack_call(text_rows, image_rows, text_lse, image_lse)
    t1a = permute(text_a, "y", 4, 1)
    t2b = permute(text_b, "y", 4, 3)
    t1b = permute(text_b, "y", 4, 1)
    t2a = permute(text_a, "y", 4, 3)
    i1 = permute(image_msg, "xl", 2, 1)
    zi0, ri0, zt0, rt0 = own_call(image_rows, text_rows, image_head, text_head)
    t1a, t2b, zi0, ri0, zt0, rt0 = lax.optimization_barrier((t1a, t2b, zi0, ri0, zt0, rt0))
    t3a = permute(t1a, "y", 4, 1)
    t3b = permute(t2b, "y", 4, 3)

    tbase, p1, p2, ri1, zi1, ig, wt = first_call(
        i1, text_rows, t1a, t1b, t2a, t2b, ri0, rt0, zt0, image_lse, text_lse, image_head, text_head
    )
    up, down, ipart, ibase, send, keep = second_call(
        core, image_rows, i1, t3a, t3b, p1, p2, ri0, ri1, zi0, zi1, ig, wt, image_lse, text_head
    )
    part = reduce_heads(send, keep)
    up, down, ipart = permute(up, "y", 4, 1), permute(down, "y", 4, 3), permute(ipart, "xl", 2, 1)
    whole, up, down, ipart = spread_heads(part, up, down, ipart)
    top, bottom = permute(up[ROWS:], "y", 4, 1), permute(down[ROWS:], "y", 4, 3)
    text_back = back_call(zt0, text_head, tbase, [up, down], [top, bottom])
    image_back = back_call(zi0, image_head, ibase, [ipart])
    whole, text_back, image_back = lax.optimization_barrier((whole, text_back, image_back))
    other = permute(whole, "core", 2, 1)
    image_total, text_total = final_call(core, other, *final_call(core, whole))
    return (image_back[None], text_back[None], image_total, text_total)


def solution(mesh):
    finer = Mesh(mesh.devices.reshape(4, 2, 4, 2, 2), BLK + REP)
    return jax.shard_map(
        shards,
        mesh=finer,
        in_specs=(P(REP, BLK, None), P(REP, BLK, None), P(), P(), P(REP, BLK), P(REP, BLK)),
        out_specs=(P(REP, BLK, None), P(REP, BLK, None), P(), P()),
        check_vma=False,
    )
```
